128 devices in a mesh: seq: 8 (over y_hi, z), head: 16 (over y_lo, x, core).
Axes of the slice: x: 4, y: 4 (y_hi: 2, y_lo: 2; y = y_hi * 2 + y_lo), z: 4, core: 2. Of those that a mesh axis runs over, the one named last changes fastest.
Arguments:
- passages: bfloat16 [2048, 8192], P('seq', 'head'), may hold values from -6 to 6
- w_query: bfloat16 [8192, 8192], P(None, 'head'), as said below
- w_key: bfloat16 [8192, 1024], P(None, 'head'), as said below
- w_value: bfloat16 [8192, 1024], P(None, 'head'), may hold values from -0.0625 to 0.0625
- w_out: bfloat16 [8192, 8192], P('head'), may hold values from -0.0625 to 0.0625
- dec_hidden: bfloat16 [32, 4, 8192], P('seq'), may hold values from -6 to 6
- cache_keys: bfloat16 [32, 16, 2048, 128], P('seq', 'head'), may hold values from -6 to 6
- cache_values: bfloat16 [32, 16, 2048, 128], P('seq', 'head'), may hold values from -6 to 6
- cache_lengths: int32 [32], P('seq'), may hold values from 1 to 4096, as said below
- assignment: int32 [32], P('seq'), may hold values from 0 to 3
Outputs:
- p_out: bfloat16 [2048, 8192], P(('seq', 'head'))
- dec_out: bfloat16 [32, 4, 8192], P('seq')
The draws below stay inside these ranges and needn't reach their ends.
Inputs may be any that keep to these rules, and one draw needn't show every extreme that they name: `cache_lengths`: some request has all 4096 slots live. `w_query`: entries lie within 4 * 8192 ** -0.5 of zero. `w_key`: entries lie within 6 * 8192 ** -0.5 of zero.
All inputs are finite; a program needn't handle non-finite values.
Results may differ from the reference program's by a relative error of at most 0.023.
Values may be sent and summed in bfloat16 or wider, within the bound.
A program may use at most 128 MiB of HBM per device.

```python
import math
import jax
import jax.numpy as jnp
from jax import lax

D = 8192
HD = 128
HEADS = 64
KVH = 8
PLEN = 512
PASS_PAIR = 1
PASSAGES = 4
PTOK = 2048
REQS = 32
STEPS = 4
CTX = 4096
N_SEQ = 8


def draw_cache_lengths(key, part):
    key = jax.random.fold_in(key, 11)
    lengths = jax.random.randint(key, (REQS,), 1, CTX + 1)
    return lengths.at[0].set(CTX).astype(jnp.int32)


def plant_pairs(key, background, first):
    blocks = background.shape[0]
    block = background.shape[1]
    width = background.shape[2]
    pick_key, level_key, sign_key, noise_key = jax.random.split(key, 4)
    where_pair = jax.random.randint(pick_key, (blocks, 1), first, block - 1)
    level = 4.0 + 0.75 * jax.random.randint(level_key, (blocks, 1, 1), 0, 3).astype(jnp.float32)
    signs = jnp.where(jax.random.bernoulli(sign_key, 0.5, (blocks, 1, width)), 1.0, -1.0)
    noise = jax.random.uniform(noise_key, (blocks, block, width), minval=-0.5, maxval=0.5)
    offsets = jnp.arange(block)[None, :]
    marked = ((offsets == where_pair) | (offsets == where_pair + 1))[:, :, None]
    return jnp.where(marked, level * signs + noise, background)


def draw_passages(key, part):
    key = jax.random.fold_in(key, 5)
    back_key, plant_key = jax.random.split(key)
    shape = (PTOK // (PLEN // 2), PLEN // 2, D)
    background = jax.random.truncated_normal(back_key, -6.0, 6.0, shape)
    values = plant_pairs(plant_key, background, 0)
    return values.reshape(PTOK, D).astype(jnp.bfloat16)


def draw_dec_hidden(key, part):
    key = jax.random.fold_in(key, 6)
    back_key, plant_key = jax.random.split(key)
    shape = (REQS, STEPS, D)
    background = jax.random.truncated_normal(back_key, -6.0, 6.0, shape)
    values = plant_pairs(plant_key, background, STEPS - 2)
    return values.astype(jnp.bfloat16)


def query_base(key):
    return jax.random.truncated_normal(key, -4.0, 4.0, (D, HEADS * HD)) * D ** (-0.5)


def draw_w_query(key, part):
    base = query_base(key)
    return base.astype(jnp.bfloat16)


def draw_w_key(key, part):
    base = query_base(key)
    key = jax.random.fold_in(key, 9)
    pick_key, own_key = jax.random.split(key)
    group = HEADS // KVH
    chosen_head = jnp.arange(KVH) * group + jax.random.randint(pick_key, (KVH,), 0, group)
    columns = (chosen_head[:, None] * HD + jnp.arange(HD)[None, :]).reshape(KVH * HD)
    aligned = jnp.take(base, columns, axis=1)
    own = jax.random.truncated_normal(own_key, -4.0, 4.0, (D, KVH * HD)) * D ** (-0.5)
    return (0.8 * aligned + 0.6 * own).astype(jnp.bfloat16)


def set_ends(array, stream_key, least, largest):
    longest = array.shape.index(max(array.shape))
    spots = []
    for shift in (0, 1):
        where = [jax.random.randint(jax.random.fold_in(stream_key, axis), (), 0, length) for axis, length in enumerate(array.shape)]
        where[longest] = (where[longest] + shift) % array.shape[longest]
        spots.append(tuple(where))
    return array.at[spots[0]].set(least).at[spots[1]].set(largest)


def steps_of(stream_key, extent, cuts, low, top_value):
    loudness = 1.0
    for axis_at, blocks in cuts:
        heights = jax.random.uniform(jax.random.fold_in(jax.random.fold_in(stream_key, 6), axis_at), (blocks,), jnp.float32, low / len(cuts), top_value / len(cuts))
        loudness = loudness * jnp.repeat(jnp.exp(heights), extent[axis_at] // blocks).reshape((-1,) + (1,) * (len(extent) - 1 - axis_at))
    return loudness


def centred(rng, extent, deviation, bound, cuts=(), held_as=jnp.bfloat16):
    values = deviation * jax.random.normal(rng, extent, jnp.float32)
    if cuts:
        values = values * steps_of(rng, extent, cuts, -0.22, 0.18)
    return jnp.clip(values, -bound, bound).astype(held_as)


def setup_inputs(seed: int = 0) -> dict:
    streams_of = jax.random.split(jax.random.key(seed), 11)
    return {
        "passages": draw_passages(jax.random.fold_in(streams_of[10], 71), 0),
        "w_query": draw_w_query(jax.random.fold_in(streams_of[10], 71), 0),
        "w_key": draw_w_key(jax.random.fold_in(streams_of[10], 71), 0),
        "w_value": centred(streams_of[3], (D, KVH * HD), D ** -0.5, 0.0625, ((1, 16),)),
        "w_out": centred(streams_of[4], (HEADS * HD, D), (HEADS * HD) ** -0.5, 0.0625, ((0, 16),)),
        "dec_hidden": draw_dec_hidden(jax.random.fold_in(streams_of[10], 71), 0),
        "cache_keys": centred(streams_of[6], (REQS, 2 * KVH, CTX // 2, HD), 1.0, 6.0, ((0, 8), (1, 16))),
        "cache_values": centred(streams_of[7], (REQS, 2 * KVH, CTX // 2, HD), 1.0, 6.0, ((0, 8), (1, 16))),
        "cache_lengths": draw_cache_lengths(jax.random.fold_in(streams_of[10], 71), 0),
        "assignment": set_ends(jax.random.randint(streams_of[9], (REQS,), 0, PASSAGES), jax.random.fold_in(streams_of[9], 1), 0, PASSAGES - 1).astype(jnp.int32),
    }


def reference(passages, w_query, w_key, w_value, w_out, dec_hidden, cache_keys, cache_values, cache_lengths, assignment):
    group_size = HEADS // KVH
    scaling = 1.0 / math.sqrt(HD)
    half_len = PLEN // 2
    pas = passages.reshape(N_SEQ // 2, 2, PASS_PAIR, half_len, D).transpose(0, 2, 1, 3, 4).reshape(PASSAGES, PLEN, D)
    causal = jnp.arange(PLEN)[:, None] >= jnp.arange(PLEN)[None, :]

    def one_passage(tokens):
        query = jnp.dot(tokens, w_query, preferred_element_type=jnp.float32).astype(jnp.bfloat16).reshape(PLEN, KVH, group_size, HD)
        keyed = jnp.dot(tokens, w_key, preferred_element_type=jnp.float32).astype(jnp.bfloat16).reshape(PLEN, KVH, HD)
        valued = jnp.dot(tokens, w_value, preferred_element_type=jnp.float32).astype(jnp.bfloat16).reshape(PLEN, KVH, HD)
        scores = jnp.einsum('tkgd,ukd->kgtu', query.astype(jnp.float32), keyed.astype(jnp.float32)) * scaling
        scores = jnp.where(causal, scores, -1e+30)
        weights = jax.nn.softmax(scores, axis=-1).astype(jnp.bfloat16)
        context = jnp.einsum('kgtu,ukd->tkgd', weights.astype(jnp.float32), valued.astype(jnp.float32)).astype(jnp.bfloat16)
        output = jnp.dot(context.reshape(PLEN, HEADS * HD), w_out, preferred_element_type=jnp.float32).astype(jnp.bfloat16)
        return (output, keyed, valued)
    outputs, pas_keys, pas_values = lax.map(one_passage, pas)
    p_out = outputs.reshape(N_SEQ // 2, PASS_PAIR, 2, half_len, D).transpose(0, 2, 1, 3, 4).reshape(PTOK, D)
    flat = dec_hidden.reshape(REQS * STEPS, D)
    dec_q = jnp.dot(flat, w_query, preferred_element_type=jnp.float32).astype(jnp.bfloat16).reshape(REQS, STEPS, KVH, group_size, HD)
    dec_k = jnp.dot(flat, w_key, preferred_element_type=jnp.float32).astype(jnp.bfloat16).reshape(REQS, STEPS, KVH, HD)
    dec_v = jnp.dot(flat, w_value, preferred_element_type=jnp.float32).astype(jnp.bfloat16).reshape(REQS, STEPS, KVH, HD)
    chosen_k = pas_keys[assignment]
    chosen_v = pas_values[assignment]
    slot_keys = cache_keys.reshape(REQS, KVH, 2, CTX // 2, HD).reshape(REQS, KVH, CTX, HD).transpose(0, 2, 1, 3)
    slot_values = cache_values.reshape(REQS, KVH, 2, CTX // 2, HD).reshape(REQS, KVH, CTX, HD).transpose(0, 2, 1, 3)
    all_keys = jnp.concatenate([chosen_k, slot_keys, dec_k], axis=1)
    all_values = jnp.concatenate([chosen_v, slot_values, dec_v], axis=1)
    scores = jnp.einsum('rskgd,rckd->rskgc', dec_q.astype(jnp.float32), all_keys.astype(jnp.float32)) * scaling
    live_pass = jnp.ones((REQS, STEPS, PLEN), dtype=bool)
    live_cache = jnp.broadcast_to((jnp.arange(CTX)[None, :] < cache_lengths[:, None])[:, None, :], (REQS, STEPS, CTX))
    live_new = jnp.broadcast_to((jnp.arange(STEPS)[None, :] <= jnp.arange(STEPS)[:, None])[None], (REQS, STEPS, STEPS))
    allowed = jnp.concatenate([live_pass, live_cache, live_new], axis=-1)[:, :, None, None, :]
    scores = jnp.where(allowed, scores, -1e+30)
    weights = jax.nn.softmax(scores, axis=-1).astype(jnp.bfloat16)
    context = jnp.einsum('rskgc,rckd->rskgd', weights.astype(jnp.float32), all_values.astype(jnp.float32)).astype(jnp.bfloat16)
    dec_out = jnp.dot(context.reshape(REQS * STEPS, HEADS * HD), w_out, preferred_element_type=jnp.float32).astype(jnp.bfloat16)
    return (p_out, dec_out.reshape(REQS, STEPS, D))
```

```python
import functools
import math

import jax
import jax.numpy as jnp
from jax import lax
from jax.experimental import pallas as pl
from jax.experimental.pallas import tpu as pltpu
from jax.sharding import PartitionSpec as P

MESH = pl.DeviceIdType.MESH
F32 = jnp.float32
BF16 = jnp.bfloat16
HD = 128
TOK = 256
DEC = 16
NEG = -1e30
ROWS = ((0, 64), (64, 64), (128, 64), (192, 64))
HALF = ((0, 128), (128, 128))


def message_ids():
    names = []
    for p in range(4):
        names += [("xp", p), ("xm", p), ("y", p)]
    names += [("xpf", 0), ("xpf", 2), ("xmf", 1), ("xmf", 3)]
    names += [("yf", dx, p) for dx in (1, 2, 3) for p in (0, 1)]
    names += [(n, p) for n in ("xpy", "xmy") for p in (2, 3)]
    names += [("xpfy", 2), ("xmfy", 3)]
    names += [("c", dx, dy, a) for dx in range(4) for dy in range(2) for a in range(2)]
    names += [("wo", i) for i in range(4)]
    names += ["kvh", "dq", "swap"]
    names += [("ctx", i) for i in range(4)]
    names += [("m1", i) for i in range(4)] + [("m2", i) for i in range(4)] + [("m3", i) for i in range(4)]
    names += [("ry", i) for i in range(4)]
    names += [("fin", i) for i in range(4)]
    names += ["part", "dctx", "dall"]
    names += [("dr", i) for i in range(1, 8)] + [("db", i) for i in range(1, 8)]
    return {n: i for i, n in enumerate(names)}


IDS = message_ids()
COUNT = len(IDS)


def dot(a, b):
    return jnp.dot(a, b, preferred_element_type=F32)


def dot_t(a, b):
    return lax.dot_general(a, b, (((1,), (1,)), ((), ())), preferred_element_type=F32)


def kernel(
    pas, wq_any, wk_any, wv_any, wo_any, dec_any, ck_any, cv_any, len_ref, asg_ref,
    pout, dout,
    xg, wq, wk, wv, wo, dech, ck, cv,
    accq, acck, accv, qb, kvh, kvo, dqo, kv, kvprev, kvall, dkv,
    ctx, part, ray, rax, rbx, rby, fin, finr,
    pk, pko, dctx, dpart, dr, dfull,
    ssem, rsem, lsem, gs, gr,
):
    s = lax.axis_index("seq")
    h = lax.axis_index("head")
    c = lax.rem(h, 2)
    chip = lax.div(h, 2)
    x = lax.rem(chip, 4)
    yl = lax.div(chip, 4)
    scale = 1.0 / math.sqrt(HD)

    def chip_at(dx, dy):
        return lax.rem(yl + dy, 2) * 4 + lax.rem(x + dx, 4)

    def dev(dx, dy, dc=0):
        return (s, chip_at(dx, dy) * 2 + lax.rem(c + dc, 2))

    XP, XM, YN, CN = dev(1, 0), dev(3, 0), dev(0, 1), dev(0, 0, 1)
    swap_dev = (s + 1 - 2 * lax.rem(s, 2), h)
    sent = []

    def send(name, src, dst, to):
        m = IDS[name]
        cp = pltpu.make_async_remote_copy(
            src_ref=src, dst_ref=dst, send_sem=ssem.at[m], recv_sem=rsem.at[m],
            device_id=to, device_id_type=MESH,
        )
        cp.start()
        sent.append(cp)

    def recv(name, ref):
        m = IDS[name]
        pltpu.make_async_remote_copy(
            src_ref=ref, dst_ref=ref, send_sem=ssem.at[m], recv_sem=rsem.at[m],
            device_id=CN, device_id_type=MESH,
        ).wait_recv()

    other = 1 - c

    def xs(dx, dy, rows, core):
        return xg.at[
            chip_at(dx, dy), pl.ds(rows[0], rows[1]), pl.ds(pl.multiple_of(core * 512, 512), 512)
        ]

    def local(i, src, dst):
        cp = pltpu.make_async_copy(src, dst, lsem.at[i])
        cp.start()
        return cp

    l_pas = local(0, pas, xs(0, 0, (0, TOK), c))
    l_dec = local(1, dec_any, dech)
    l_wq = local(2, wq_any, wq)
    l_wk = local(3, wk_any, wk)
    l_wv = local(4, wv_any, wv)

    barrier = pltpu.get_barrier_semaphore()
    plane = [(dx, dy) for dy in range(2) for dx in range(4) if (dx, dy) != (0, 0)]
    for dx, dy in plane:
        pl.semaphore_signal(barrier, inc=1, device_id=dev(dx, dy), device_id_type=MESH)
    pl.semaphore_signal(barrier, inc=1, device_id=CN, device_id_type=MESH)
    for d in range(1, 8):
        pl.semaphore_signal(barrier, inc=1, device_id=(lax.rem(s + d, 8), h), device_id_type=MESH)
    pl.semaphore_wait(barrier, 15)

    for a, b, e in ((0, 1, 2), (1, 0, 3), (2, 3, 0), (3, 2, 1)):
        send(("xp", a), pas.at[pl.ds(*ROWS[a])], xs(0, 0, ROWS[a], c), XP)
        send(("xm", b), pas.at[pl.ds(*ROWS[b])], xs(0, 0, ROWS[b], c), XM)
        send(("y", e), pas.at[pl.ds(*ROWS[e])], xs(0, 0, ROWS[e], c), YN)
    for a in range(2):
        send(("c", 0, 0, a), pas.at[pl.ds(*HALF[a])], xs(0, 0, HALF[a], c), CN)

    def fwd(name, dx, dy, rows, to):
        ref = xs(dx, dy, rows, c)
        send(name, ref, ref, to)

    def got(name, dx, dy, rows):
        recv(name, xs(dx, dy, rows, c))

    def share(dx, dy, a):
        fwd(("c", dx, dy, a), dx, dy, HALF[a], CN)

    def shared(dx, dy):
        for a in range(2):
            recv(("c", dx, dy, a), xs(dx, dy, HALF[a], other))

    l_wo = local(5, wo_any.at[:, pl.ds(pl.multiple_of(c * 4096, 4096), 4096)], wo.at[c])
    l_ck = local(6, ck_any, ck)
    l_cv = local(7, cv_any, cv)

    def push_wo(i):
        send(
            ("wo", i),
            wo_any.at[pl.ds(i * 128, 128), pl.ds(pl.multiple_of(other * 4096, 4096), 4096)],
            wo.at[c, pl.ds(i * 128, 128), :],
            CN,
        )

    l_dec.wait()
    for j in range(8):
        rows = dech[:, :, j * 1024 : (j + 1) * 1024].astype(F32).reshape(DEC, 1024)
        xg[j, TOK:, :] = rows.astype(BF16)
    accq[...] = jnp.zeros_like(accq)
    acck[...] = jnp.zeros_like(acck)
    accv[...] = jnp.zeros_like(accv)

    def project_kv(dx, dy):
        j = chip_at(dx, dy)
        rows = pl.ds(pl.multiple_of(j * 1024, 1024), 1024)
        acck[...] += dot(xg[j], wk[rows, :])
        accv[...] += dot(xg[j], wv[rows, :])

    def project_q(dx, dy):
        j = chip_at(dx, dy)
        rows = pl.ds(pl.multiple_of(j * 1024, 1024), 1024)
        accq[...] += dot(xg[j], wq[rows, :])

    def project(dx, dy):
        shared(dx, dy)
        project_kv(dx, dy)
        project_q(dx, dy)

    got(("xp", 0), 3, 0, ROWS[0])
    fwd(("xpf", 0), 3, 0, ROWS[0], XP)
    fwd(("yf", 3, 0), 3, 0, ROWS[0], YN)
    got(("xm", 1), 1, 0, ROWS[1])
    fwd(("xmf", 1), 1, 0, ROWS[1], XM)
    fwd(("yf", 1, 1), 1, 0, ROWS[1], YN)
    for p in (2, 3):
        got(("y", p), 0, 1, ROWS[p])
        fwd(("xpy", p), 0, 1, ROWS[p], XP)
        fwd(("xmy", p), 0, 1, ROWS[p], XM)
    share(0, 1, 1)
    got(("xp", 1), 3, 0, ROWS[1])
    fwd(("yf", 3, 1), 3, 0, ROWS[1], YN)
    got(("xm", 0), 1, 0, ROWS[0])
    fwd(("yf", 1, 0), 1, 0, ROWS[0], YN)
    share(3, 0, 0)
    share(1, 0, 0)
    push_wo(0)
    l_pas.wait()
    l_wq.wait()
    l_wk.wait()
    l_wv.wait()
    project(0, 0)
    got(("xp", 2), 3, 0, ROWS[2])
    fwd(("xpf", 2), 3, 0, ROWS[2], XP)
    got(("xm", 3), 1, 0, ROWS[3])
    fwd(("xmf", 3), 1, 0, ROWS[3], XM)
    got(("xpf", 0), 2, 0, ROWS[0])
    fwd(("yf", 2, 0), 2, 0, ROWS[0], YN)
    got(("xmf", 1), 2, 0, ROWS[1])
    fwd(("yf", 2, 1), 2, 0, ROWS[1], YN)
    share(2, 0, 0)
    got(("xp", 3), 3, 0, ROWS[3])
    share(3, 0, 1)
    got(("xm", 2), 1, 0, ROWS[2])
    share(1, 0, 1)
    push_wo(1)
    project(3, 0)
    got(("y", 0), 0, 1, ROWS[0])
    got(("y", 1), 0, 1, ROWS[1])
    share(0, 1, 0)
    project(1, 0)
    push_wo(2)
    got(("xpy", 2), 3, 1, ROWS[2])
    fwd(("xpfy", 2), 3, 1, ROWS[2], XP)
    got(("xmy", 3), 1, 1, ROWS[3])
    fwd(("xmfy", 3), 1, 1, ROWS[3], XM)
    project(0, 1)
    push_wo(3)
    got(("xpf", 2), 2, 0, ROWS[2])
    got(("xmf", 3), 2, 0, ROWS[3])
    share(2, 0, 1)
    project(2, 0)
    got(("xpy", 3), 3, 1, ROWS[3])
    share(3, 1, 1)
    got(("xmy", 2), 1, 1, ROWS[2])
    share(1, 1, 1)
    got(("yf", 3, 0), 3, 1, ROWS[0])
    got(("yf", 3, 1), 3, 1, ROWS[1])
    share(3, 1, 0)
    got(("yf", 1, 0), 1, 1, ROWS[0])
    got(("yf", 1, 1), 1, 1, ROWS[1])
    share(1, 1, 0)
    project(3, 1)
    got(("xpfy", 2), 2, 1, ROWS[2])
    got(("xmfy", 3), 2, 1, ROWS[3])
    share(2, 1, 1)
    got(("yf", 2, 0), 2, 1, ROWS[0])
    got(("yf", 2, 1), 2, 1, ROWS[1])
    share(2, 1, 0)
    project(1, 1)
    shared(2, 1)
    project_kv(2, 1)
    kvh[0] = acck[...].astype(BF16)
    kvh[1] = accv[...].astype(BF16)
    send("kvh", kvh, kvo, CN)
    project_q(2, 1)
    qb[...] = accq[...].astype(BF16)
    send("dq", qb.at[pl.ds(TOK, DEC)], dqo, CN)
    recv("kvh", kvo)
    low = c == 0
    for i in range(2):
        mine = kvh[i].astype(F32)
        theirs = kvo[i].astype(F32)
        full = jnp.where(
            low,
            jnp.concatenate([mine, theirs], axis=1),
            jnp.concatenate([theirs, mine], axis=1),
        ).astype(BF16)
        kv[i] = full[:TOK]
        dkv[i] = full[TOK:]
    send("swap", kv, kvprev, swap_dev)
    mine_parity = lax.rem(s, 2) == c
    slot = lax.div(s, 2)

    def gather_copy(d):
        return pltpu.make_async_remote_copy(
            src_ref=kv, dst_ref=kvall.at[slot], send_sem=gs.at[d], recv_sem=gr.at[slot],
            device_id=(lax.rem(s + d, 8), h), device_id_type=MESH,
        )

    @pl.when(mine_parity)
    def _():
        for d in range(1, 8):
            gather_copy(d).start()
        kvall[slot] = kv[...]

    recv("swap", kvprev)
    second = lax.rem(s, 2) == 1
    row = lax.broadcasted_iota(jnp.int32, (TOK, TOK), 0)
    col = lax.broadcasted_iota(jnp.int32, (TOK, TOK), 1)
    for i in range(4):
        q = qb[0:TOK, i * HD : (i + 1) * HD]
        s1 = jnp.where(row >= col, dot_t(q, kv[0]) * scale, NEG)
        s0 = jnp.where(second, dot_t(q, kvprev[0]) * scale, NEG)
        m = jnp.maximum(jnp.max(s1, axis=1, keepdims=True), jnp.max(s0, axis=1, keepdims=True))
        e1 = jnp.exp(s1 - m)
        e0 = jnp.exp(s0 - m)
        inv = 1.0 / (jnp.sum(e1, axis=1, keepdims=True) + jnp.sum(e0, axis=1, keepdims=True))
        o = dot((e1 * inv).astype(BF16), kv[1]) + dot((e0 * inv).astype(BF16), kvprev[1])
        ctx[c, :, i * HD : (i + 1) * HD] = o.astype(BF16)
        ref = ctx.at[c, :, pl.ds(i * HD, HD)]
        send(("ctx", i), ref, ref, CN)

    l_wo.wait()
    for i in range(4):
        recv(("wo", i), wo.at[other, pl.ds(i * 128, 128), :])
    for i in range(4):
        recv(("ctx", i), ctx.at[other, :, pl.ds(i * HD, HD)])

    def along(f):
        return (XP, XM) if f == 1 else (XM, XP)

    def at_x(d):
        return lax.rem(x + d, 4)

    far = 1 - yl
    FLOW = {0: 1, 1: 3, 2: 1, 3: 3}

    def x_block(ci, d):
        if ci < 2:
            return part.at[ci, yl, at_x(d)]
        return part.at[ci, :, at_x(d)]

    def x_land(ci, k):
        return rax.at[ci, k] if ci < 2 else rbx.at[ci - 2, k]

    def x_start(ci):
        f = FLOW[ci]
        ahead, behind = along(f)
        send(("m1", ci), x_block(ci, 2), x_land(ci, 0), ahead)
        send(("m2", ci), x_block(ci, 4 - f), x_land(ci, 1), behind)

    def x_pass(ci):
        f = FLOW[ci]
        ahead, _ = along(f)
        recv(("m1", ci), x_land(ci, 0))
        block = x_block(ci, f)
        block[...] = (block[...].astype(F32) + x_land(ci, 0)[...].astype(F32)).astype(BF16)
        send(("m3", ci), block, x_land(ci, 2), ahead)

    def x_end(ci):
        recv(("m2", ci), x_land(ci, 1))
        recv(("m3", ci), x_land(ci, 2))
        return (
            x_block(ci, 0)[...].astype(F32)
            + x_land(ci, 1)[...].astype(F32)
            + x_land(ci, 2)[...].astype(F32)
        )

    for ci in (0, 2, 1, 3):
        cols = slice(ci * 1024, (ci + 1) * 1024)
        total = dot(ctx[0], wo[0, :, cols]) + dot(ctx[1], wo[1, :, cols])
        part[ci] = total.astype(BF16).reshape(2, 4, 32, 1024)
        if ci < 2:
            send(("ry", ci), part.at[ci, far], ray.at[ci], YN)
        else:
            x_start(ci)

    recv("dq", dqo)
    own_q = qb[TOK:, :]
    other_q = dqo[...]
    q_low = jnp.where(low, own_q.astype(F32), other_q.astype(F32)).astype(BF16)
    q_high = jnp.where(low, other_q.astype(F32), own_q.astype(F32)).astype(BF16)
    q_all = jnp.concatenate(
        [t[:, i * HD : (i + 1) * HD] for t in (q_low, q_high) for i in range(4)], axis=0
    )
    to = lax.broadcasted_iota(jnp.int32, (128, 128), 0)
    frm = lax.broadcasted_iota(jnp.int32, (128, 128), 1)
    source = (to // 64) * 64 + ((to % 16) // 4) * 16 + ((to % 64) // 16) * 4 + to % 4
    q_rows = dot((source == frm).astype(BF16), q_all).astype(BF16)

    l_ck.wait()
    l_cv.wait()

    def decode(r):
        q = jnp.concatenate([q_rows[r * 16 : r * 16 + 16], q_rows[64 + r * 16 : 80 + r * 16]], axis=0)
        pkv = kvall[asg_ref[r]]
        sc = dot_t(q, ck[r, 0]) * scale
        place = c * 2048 + lax.broadcasted_iota(jnp.int32, sc.shape, 1)
        sc = jnp.where(place < len_ref[r], sc, NEG)
        sp = dot_t(q, pkv[0]) * scale
        sn = dot_t(q, dkv[0]) * scale
        step = lax.broadcasted_iota(jnp.int32, sn.shape, 0) % 4
        new = lax.broadcasted_iota(jnp.int32, sn.shape, 1)
        sn = jnp.where(low & (new // 4 == r) & (new % 4 <= step), sn, NEG)
        m = jnp.maximum(
            jnp.max(sc, axis=1, keepdims=True),
            jnp.maximum(jnp.max(sp, axis=1, keepdims=True), jnp.max(sn, axis=1, keepdims=True)),
        )
        ec, ep, en = jnp.exp(sc - m), jnp.exp(sp - m), jnp.exp(sn - m)
        l = (
            jnp.sum(ec, axis=1, keepdims=True)
            + jnp.sum(ep, axis=1, keepdims=True)
            + jnp.sum(en, axis=1, keepdims=True)
        )
        o = dot(ec.astype(BF16), cv[r, 0]) + dot(ep.astype(BF16), pkv[1]) + dot(en.astype(BF16), dkv[1])
        for half in range(2):
            t = slice(half * 16, half * 16 + 16)
            pk[half, 0, r * 16 : r * 16 + 16] = o[t]
            pk[half, 1, r * 16 : r * 16 + 16] = jnp.broadcast_to(m[t], (16, HD))
            pk[half, 2, r * 16 : r * 16 + 16] = jnp.broadcast_to(l[t], (16, HD))

    x_pass(2)
    x_pass(3)
    for j in range(4):
        @pl.when(2 * j + c != s)
        def _():
            pltpu.make_async_remote_copy(
                src_ref=kv, dst_ref=kvall.at[j], send_sem=gs.at[0], recv_sem=gr.at[j],
                device_id=CN, device_id_type=MESH,
            ).wait_recv()

    decode(0)
    decode(1)
    for ci in range(2):
        recv(("ry", ci), ray.at[ci])
        part[ci, yl] = (part[ci, yl].astype(F32) + ray[ci].astype(F32)).astype(BF16)
        x_start(ci)
    decode(2)
    decode(3)
    send("part", pk.at[other], pko, CN)
    x_pass(0)
    x_pass(1)
    recv("part", pko)
    o1, m1, l1 = pk[c, 0], pk[c, 1], pk[c, 2]
    o2, m2, l2 = pko[0], pko[1], pko[2]
    mm = jnp.maximum(m1, m2)
    a1, a2 = jnp.exp(m1 - mm), jnp.exp(m2 - mm)
    dec_ctx = ((a1 * o1 + a2 * o2) / (a1 * l1 + a2 * l2)).astype(BF16)
    to = lax.broadcasted_iota(jnp.int32, (16, 64), 0)
    frm = lax.broadcasted_iota(jnp.int32, (16, 64), 1)
    for i in range(4):
        pick = ((to // 4) * 16 + i * 4 + to % 4 == frm).astype(BF16)
        dctx[c, :, i * HD : (i + 1) * HD] = dot(pick, dec_ctx).astype(BF16)
    send("dctx", dctx.at[c], dctx.at[c], CN)

    for ci in (2, 3):
        rbx[ci - 2, 1] = x_end(ci).astype(BF16)
        send(("ry", ci), rbx.at[ci - 2, 1, far], rby.at[ci - 2], YN)

    recv("dctx", dctx.at[other])
    for j in range(8):
        cols = slice(j * 512, (j + 1) * 512)
        dpart[j] = (dot(dctx[0], wo[0, :, cols]) + dot(dctx[1], wo[1, :, cols])).astype(BF16)
    for i in range(1, 8):
        dx, dy = i % 4, i // 4
        send(("dr", i), dpart.at[chip_at(dx, dy)], dr.at[i], dev(dx, dy))

    def finish(ci, total):
        fin[ci] = total.astype(BF16)
        send(
            ("fin", ci),
            fin.at[ci, pl.ds(pl.multiple_of(other * 16, 16), 16)],
            finr.at[ci],
            CN,
        )

    for ci in range(2):
        finish(ci, x_end(ci))

    total = dpart[chip].astype(F32)
    for i in range(1, 8):
        recv(("dr", i), dr.at[i])
        total = total + dr[i].astype(F32)
    dfull[c, chip] = total.astype(BF16)
    for i in range(1, 8):
        dx, dy = i % 4, i // 4
        ref = dfull.at[c, chip]
        send(("db", i), ref, ref, dev(dx, dy))

    for ci in (2, 3):
        recv(("ry", ci), rby.at[ci - 2])
        finish(ci, rbx[ci - 2, 1, yl].astype(F32) + rby[ci - 2].astype(F32))

    for i in range(1, 8):
        dx, dy = i % 4, i // 4
        recv(("db", i), dfull.at[c, chip_at(4 - dx, dy)])
    send("dall", dfull.at[c], dfull.at[c], CN)
    base = pl.multiple_of(c * 4096, 4096)
    far_base = pl.multiple_of(other * 4096, 4096)
    for ci in range(4):
        keep = fin[ci, pl.ds(pl.multiple_of(c * 16, 16), 16), :]
        pout[:, pl.ds(base + ci * 1024, 1024)] = keep
    for ci in range(4):
        recv(("fin", ci), finr.at[ci])
        pout[:, pl.ds(far_base + ci * 1024, 1024)] = finr[ci]
    recv("dall", dfull.at[other])
    for a in range(2):
        for j in range(8):
            at = a * 4096 + j * 512
            dout[:, at : at + 512] = dfull[a, j]

    for cp in sent:
        cp.wait_send()

    @pl.when(mine_parity)
    def _():
        for d in range(1, 8):
            gather_copy(d).wait_send()


def local(
    passages, w_query, w_key, w_value, w_out, dec_hidden, cache_keys, cache_values, cache_lengths, assignment
):
    any_spec = pl.BlockSpec(memory_space=pl.ANY)
    smem = pl.BlockSpec(memory_space=pltpu.SMEM)
    vmem = pl.BlockSpec(memory_space=pltpu.VMEM)
    V = pltpu.VMEM
    p_out, dec_out = pl.pallas_call(
        kernel,
        out_shape=(
            jax.ShapeDtypeStruct((16, 8192), BF16),
            jax.ShapeDtypeStruct((DEC, 8192), BF16),
        ),
        in_specs=[any_spec] * 8 + [smem] * 2,
        out_specs=(vmem, vmem),
        scratch_shapes=[
            V((8, TOK + DEC, 1024), BF16),
            V((8192, 512), BF16),
            V((8192, 64), BF16),
            V((8192, 64), BF16),
            V((2, 512, 4096), BF16),
            V((4, 4, 8192), BF16),
            V((4, 1, 2048, HD), BF16),
            V((4, 1, 2048, HD), BF16),
            V((TOK + DEC, 512), F32),
            V((TOK + DEC, 64), F32),
            V((TOK + DEC, 64), F32),
            V((TOK + DEC, 512), BF16),
            V((2, TOK + DEC, 64), BF16),
            V((2, TOK + DEC, 64), BF16),
            V((DEC, 512), BF16),
            V((2, TOK, HD), BF16),
            V((2, TOK, HD), BF16),
            V((4, 2, TOK, HD), BF16),
            V((2, DEC, HD), BF16),
            V((2, TOK, 512), BF16),
            V((4, 2, 4, 32, 1024), BF16),
            V((2, 4, 32, 1024), BF16),
            V((2, 3, 32, 1024), BF16),
            V((2, 3, 2, 32, 1024), BF16),
            V((2, 32, 1024), BF16),
            V((4, 32, 1024), BF16),
            V((4, 16, 1024), BF16),
            V((2, 3, 64, HD), F32),
            V((3, 64, HD), F32),
            V((2, DEC, 512), BF16),
            V((8, DEC, 512), BF16),
            V((8, DEC, 512), BF16),
            V((2, 8, DEC, 512), BF16),
            pltpu.SemaphoreType.DMA((COUNT,)),
            pltpu.SemaphoreType.DMA((COUNT,)),
            pltpu.SemaphoreType.DMA((8,)),
            pltpu.SemaphoreType.DMA((8,)),
            pltpu.SemaphoreType.DMA((4,)),
        ],
        compiler_params=pltpu.CompilerParams(
            collective_id=0, has_side_effects=True, vmem_limit_bytes=60 * 2**20
        ),
        name="layer",
    )(
        passages, w_query, w_key, w_value, w_out, dec_hidden, cache_keys, cache_values, cache_lengths, assignment
    )
    return p_out, dec_out.reshape(4, 4, 8192)


def solution(mesh):
    in_specs = (
        P("seq", "head"),
        P(None, "head"),
        P(None, "head"),
        P(None, "head"),
        P("head", None),
        P("seq", None, None),
        P("seq", "head", None, None),
        P("seq", "head", None, None),
        P("seq"),
        P("seq"),
    )
    out_specs = (P(("seq", "head"), None), P("seq", None, None))
    return jax.shard_map(local, mesh=mesh, in_specs=in_specs, out_specs=out_specs, check_vma=False)
```

```python
import functools
import math

import jax
import jax.numpy as jnp
from jax import lax
from jax.experimental import pallas as pl
from jax.experimental.pallas import tpu as pltpu
from jax.sharding import PartitionSpec as P

MESH = pl.DeviceIdType.MESH
F32 = jnp.float32
BF16 = jnp.bfloat16
HD = 128
TOK = 256
DEC = 16
NEG = -1e30
ROWS = ((0, 64), (64, 48), (112, 64), (176, 80))
HALF = ((0, 112), (112, 144))
WA, WB = 384, 640
WO_PIECES = 8


def message_ids():
    names = []
    for p in range(4):
        names += [("xp", p), ("xm", p), ("y", p)]
    names += [("xpf", 0), ("xpf", 2), ("xmf", 1), ("xmf", 3)]
    names += [("yf", dx, p) for dx in (1, 2, 3) for p in (0, 1)]
    names += [(n, p) for n in ("xpy", "xmy") for p in (2, 3)]
    names += [("xpfy", 2), ("xmfy", 3)]
    names += [("c", dx, dy, a) for dx in range(4) for dy in range(2) for a in range(2)]
    names += [("wo", i) for i in range(WO_PIECES)]
    names += ["wk", "wv", "dq", "swapk", "swapv"]
    names += [("ctx", i) for i in range(4)]
    names += [(n, i) for n in ("m1", "m2", "m3", "ry", "fin") for i in range(8)]
    names += ["part", "dctx", "dall"]
    names += [("dr", i) for i in range(1, 8)] + [("db", i) for i in range(1, 8)]
    return {n: i for i, n in enumerate(names)}


IDS = message_ids()
COUNT = len(IDS)


def dot(a, b):
    return jnp.dot(a, b, preferred_element_type=F32)


def dot_t(a, b):
    return lax.dot_general(a, b, (((1,), (1,)), ((), ())), preferred_element_type=F32)


def rowmax(a):
    return jnp.max(a, axis=1, keepdims=True)


def rowsum(a):
    return jnp.sum(a, axis=1, keepdims=True)


def kernel(
    pas, wq_any, wk_any, wv_any, wo_any, dec_any, ck_any, cv_any, len_ref, asg_ref,
    pout, dout,
    xg, xd, wq, wkv, wo, dech, ck, cv,
    accq, acckv, accdq, accdkv, qb, dqb, dqo, kv, kvprev, kvall, dkv,
    ctx, parta, partb, ray, rax, rbx, rby, fina, finb, finra, finrb,
    pc, pk, pko, dctx, dpart, dr, dfull,
    ssem, rsem, lsem, gs, gr,
):
    s = lax.axis_index("seq")
    h = lax.axis_index("head")
    c = lax.rem(h, 2)
    other = 1 - c
    chip = lax.div(h, 2)
    x = lax.rem(chip, 4)
    yl = lax.div(chip, 4)
    low = c == 0
    scale = 1.0 / math.sqrt(HD)

    def chip_at(dx, dy):
        return lax.rem(yl + dy, 2) * 4 + lax.rem(x + dx, 4)

    def dev(dx, dy, dc=0):
        return (s, chip_at(dx, dy) * 2 + lax.rem(c + dc, 2))

    XP, XM, YN, CN = dev(1, 0), dev(3, 0), dev(0, 1), dev(0, 0, 1)
    swap_dev = (s + 1 - 2 * lax.rem(s, 2), h)
    mate = lax.rem(s + 4, 8)
    sent = []

    def send(name, src, dst, to):
        m = IDS[name]
        cp = pltpu.make_async_remote_copy(
            src_ref=src, dst_ref=dst, send_sem=ssem.at[m], recv_sem=rsem.at[m],
            device_id=to, device_id_type=MESH,
        )
        cp.start()
        sent.append(cp)

    def recv(name, ref):
        m = IDS[name]
        pltpu.make_async_remote_copy(
            src_ref=ref, dst_ref=ref, send_sem=ssem.at[m], recv_sem=rsem.at[m],
            device_id=CN, device_id_type=MESH,
        ).wait_recv()

    def local(i, src, dst):
        cp = pltpu.make_async_copy(src, dst, lsem.at[i])
        cp.start()
        return cp

    def xs(dx, dy, rows, core):
        return xg.at[
            chip_at(dx, dy), pl.ds(rows[0], rows[1]), pl.ds(pl.multiple_of(core * 512, 512), 512)
        ]

    def kv_rows(i, core):
        return wkv.at[pl.ds(pl.multiple_of(i * HD + core * 64, 64), 64)]

    l_pas = local(0, pas, xs(0, 0, (0, TOK), c))
    l_dec = local(1, dec_any, dech)
    l_wk = local(3, wk_any, kv_rows(0, c))
    l_wv = local(4, wv_any, kv_rows(1, c))
    l_wq = local(2, wq_any, wq)

    barrier = pltpu.get_barrier_semaphore()
    plane = [(dx, dy) for dy in range(2) for dx in range(4) if (dx, dy) != (0, 0)]
    for dx, dy in plane:
        pl.semaphore_signal(barrier, inc=1, device_id=dev(dx, dy), device_id_type=MESH)
    pl.semaphore_signal(barrier, inc=1, device_id=CN, device_id_type=MESH)
    for d in range(1, 8):
        pl.semaphore_signal(barrier, inc=1, device_id=(lax.rem(s + d, 8), h), device_id_type=MESH)
    pl.semaphore_wait(barrier, 15)

    def own(name, p, to):
        send((name, p), pas.at[pl.ds(*ROWS[p])], xs(0, 0, ROWS[p], c), to)

    def fwd(name, dx, dy, rows, to):
        ref = xs(dx, dy, rows, c)
        send(name, ref, ref, to)

    def got(name, dx, dy, rows):
        recv(name, xs(dx, dy, rows, c))

    def share(dx, dy, a):
        fwd(("c", dx, dy, a), dx, dy, HALF[a], CN)

    def shared(dx, dy):
        for a in range(2):
            recv(("c", dx, dy, a), xs(dx, dy, HALF[a], other))

    own("xp", 0, XP)
    own("xm", 1, XM)
    own("y", 2, YN)
    own("xp", 2, XP)
    own("xm", 3, XM)
    own("y", 3, YN)
    own("xp", 1, XP)
    own("xm", 0, XM)
    own("y", 0, YN)
    own("y", 1, YN)
    for a in range(2):
        send(("c", 0, 0, a), pas.at[pl.ds(*HALF[a])], xs(0, 0, HALF[a], c), CN)
    send("wk", wk_any, kv_rows(0, c), CN)
    send("wv", wv_any, kv_rows(1, c), CN)
    l_ck = local(6, ck_any, ck)
    l_cv = local(7, cv_any, cv)
    l_wo = local(5, wo_any.at[:, pl.ds(pl.multiple_of(c * 4096, 4096), 4096)], wo.at[c])

    wo_rows = 512 // WO_PIECES

    def push_wo(i):
        send(
            ("wo", i),
            wo_any.at[pl.ds(i * wo_rows, wo_rows), pl.ds(pl.multiple_of(other * 4096, 4096), 4096)],
            wo.at[c, pl.ds(i * wo_rows, wo_rows), :],
            CN,
        )

    l_dec.wait()
    for j in range(8):
        rows = dech[:, :, j * 1024 : (j + 1) * 1024].astype(F32).reshape(DEC, 1024)
        xd[j] = rows.astype(BF16)
    accq[...] = jnp.zeros_like(accq)
    acckv[...] = jnp.zeros_like(acckv)

    def project_kv(dx, dy):
        j = chip_at(dx, dy)
        cols = pl.ds(pl.multiple_of(j * 1024, 1024), 1024)
        acckv[...] += dot_t(xg[j], wkv[:, cols])

    def project_q(dx, dy):
        j = chip_at(dx, dy)
        rows = pl.ds(pl.multiple_of(j * 1024, 1024), 1024)
        accq[...] += dot(xg[j], wq[rows, :])

    def project_new(j):
        q = dot(xd[j], wq[j * 1024 : (j + 1) * 1024, :])
        k = dot_t(xd[j], wkv[:, j * 1024 : (j + 1) * 1024])
        if j == 0:
            accdq[...] = q
            accdkv[...] = k
        else:
            accdq[...] += q
            accdkv[...] += k

    got(("xm", 1), 1, 0, ROWS[1])
    fwd(("yf", 1, 1), 1, 0, ROWS[1], YN)
    fwd(("xmf", 1), 1, 0, ROWS[1], XM)
    got(("y", 2), 0, 1, ROWS[2])
    fwd(("xpy", 2), 0, 1, ROWS[2], XP)
    got(("xp", 0), 3, 0, ROWS[0])
    fwd(("yf", 3, 0), 3, 0, ROWS[0], YN)
    fwd(("xpf", 0), 3, 0, ROWS[0], XP)
    l_wk.wait()
    l_wv.wait()
    l_wq.wait()
    l_pas.wait()
    got(("y", 3), 0, 1, ROWS[3])
    fwd(("xmy", 3), 0, 1, ROWS[3], XM)
    got(("xp", 2), 3, 0, ROWS[2])
    fwd(("xpf", 2), 3, 0, ROWS[2], XP)
    fwd(("xpy", 3), 0, 1, ROWS[3], XP)
    got(("xm", 3), 1, 0, ROWS[3])
    fwd(("xmf", 3), 1, 0, ROWS[3], XM)
    fwd(("xmy", 2), 0, 1, ROWS[2], XM)
    own("xp", 3, XP)
    own("xm", 2, XM)
    share(0, 1, 1)
    got(("xp", 1), 3, 0, ROWS[1])
    fwd(("yf", 3, 1), 3, 0, ROWS[1], YN)
    share(3, 0, 0)
    got(("xm", 0), 1, 0, ROWS[0])
    fwd(("yf", 1, 0), 1, 0, ROWS[0], YN)
    share(1, 0, 0)
    recv("wk", kv_rows(0, other))
    recv("wv", kv_rows(1, other))
    push_wo(0)
    project_new(0)
    project_new(1)
    got(("xmf", 1), 2, 0, ROWS[1])
    fwd(("yf", 2, 1), 2, 0, ROWS[1], YN)
    got(("xpy", 2), 3, 1, ROWS[2])
    fwd(("xpfy", 2), 3, 1, ROWS[2], XP)
    project_new(2)
    project_new(3)
    got(("xpf", 0), 2, 0, ROWS[0])
    fwd(("yf", 2, 0), 2, 0, ROWS[0], YN)
    share(2, 0, 0)
    push_wo(1)
    got(("xmy", 3), 1, 1, ROWS[3])
    fwd(("xmfy", 3), 1, 1, ROWS[3], XM)
    got(("y", 0), 0, 1, ROWS[0])
    got(("y", 1), 0, 1, ROWS[1])
    share(0, 1, 0)
    for j in range(4, 8):
        project_new(j)
    dqb[...] = accdq[...].astype(BF16)
    send("dq", dqb, dqo, CN)
    for i in range(2):
        dkv[i] = accdkv[:, i * HD : (i + 1) * HD].astype(BF16)
    shared(0, 0)
    project_kv(0, 0)
    project_q(0, 0)
    got(("xpf", 2), 2, 0, ROWS[2])
    got(("xmf", 3), 2, 0, ROWS[3])
    share(2, 0, 1)
    push_wo(2)
    shared(0, 1)
    project_kv(0, 1)
    project_q(0, 1)
    got(("yf", 3, 0), 3, 1, ROWS[0])
    got(("yf", 1, 1), 1, 1, ROWS[1])
    got(("yf", 3, 1), 3, 1, ROWS[1])
    got(("yf", 1, 0), 1, 1, ROWS[0])
    share(3, 1, 0)
    share(1, 1, 0)
    shared(2, 0)
    project_kv(2, 0)
    project_q(2, 0)
    got(("xpy", 3), 3, 1, ROWS[3])
    share(3, 1, 1)
    got(("xmy", 2), 1, 1, ROWS[2])
    share(1, 1, 1)
    got(("xp", 3), 3, 0, ROWS[3])
    share(3, 0, 1)
    got(("xm", 2), 1, 0, ROWS[2])
    share(1, 0, 1)
    got(("xpfy", 2), 2, 1, ROWS[2])
    got(("xmfy", 3), 2, 1, ROWS[3])
    share(2, 1, 1)
    got(("yf", 2, 1), 2, 1, ROWS[1])
    got(("yf", 2, 0), 2, 1, ROWS[0])
    share(2, 1, 0)
    for place in ((3, 1), (1, 1), (3, 0), (1, 0), (2, 1)):
        shared(*place)
        project_kv(*place)

    for i in range(2):
        kv[i] = acckv[:, i * HD : (i + 1) * HD].astype(BF16)
    send("swapk", kv.at[0], kvprev.at[0], swap_dev)
    send("swapv", kv.at[1], kvprev.at[1], swap_dev)
    for i in range(3, WO_PIECES):
        push_wo(i)
    for place in ((3, 1), (1, 1), (3, 0), (1, 0), (2, 1)):
        project_q(*place)
    qb[...] = accq[...].astype(BF16)

    mine_parity = lax.rem(s, 2) == c
    slot = lax.div(s, 2)
    mate_slot = lax.div(mate, 2)

    def gather_copy(d):
        first = lax.div(s, 4) * 4
        if d == 4:
            to = mate
        else:
            to = first + lax.rem(s + d % 4, 4)
        if d < 5:
            src, at = kv, slot
        else:
            src, at = kvall.at[mate_slot], mate_slot
        return pltpu.make_async_remote_copy(
            src_ref=src, dst_ref=kvall.at[at], send_sem=gs.at[d], recv_sem=gr.at[at],
            device_id=(to, h), device_id_type=MESH,
        )

    def gather_wait(j):
        pltpu.make_async_remote_copy(
            src_ref=kv, dst_ref=kvall.at[j], send_sem=gs.at[0], recv_sem=gr.at[j],
            device_id=CN, device_id_type=MESH,
        ).wait_recv()

    @pl.when(mine_parity)
    def _():
        gather_copy(4).start()
        for d in range(1, 4):
            gather_copy(d).start()
        kvall[slot] = kv[...]

    row = lax.broadcasted_iota(jnp.int32, (TOK, TOK), 0)
    col = lax.broadcasted_iota(jnp.int32, (TOK, TOK), 1)
    held = []
    for i in range(4):
        q = qb[:, i * HD : (i + 1) * HD]
        s1 = jnp.where(row >= col, dot_t(q, kv[0]) * scale, NEG)
        m1 = rowmax(s1)
        e1 = jnp.exp(s1 - m1)
        held.append((m1, rowsum(e1), dot(e1.astype(BF16), kv[1])))

    recv("dq", dqo)
    q_low = jnp.where(low, dqb[...].astype(F32), dqo[...].astype(F32)).astype(BF16)
    q_high = jnp.where(low, dqo[...].astype(F32), dqb[...].astype(F32)).astype(BF16)
    q_all = jnp.concatenate(
        [t[:, i * HD : (i + 1) * HD] for t in (q_low, q_high) for i in range(4)], axis=0
    )
    to = lax.broadcasted_iota(jnp.int32, (128, 128), 0)
    frm = lax.broadcasted_iota(jnp.int32, (128, 128), 1)
    source = (to // 64) * 64 + ((to % 16) // 4) * 16 + ((to % 64) // 16) * 4 + to % 4
    q_rows = dot((source == frm).astype(BF16), q_all).astype(BF16)
    l_ck.wait()
    l_cv.wait()

    def new_q(r):
        return jnp.concatenate(
            [q_rows[r * 16 : r * 16 + 16], q_rows[64 + r * 16 : 80 + r * 16]], axis=0
        )

    def decode_cache(r):
        q = new_q(r)
        sc = dot_t(q, ck[r, 0]) * scale
        place = c * 2048 + lax.broadcasted_iota(jnp.int32, sc.shape, 1)
        sc = jnp.where(place < len_ref[r], sc, NEG)
        sn = dot_t(q, dkv[0]) * scale
        step = lax.broadcasted_iota(jnp.int32, sn.shape, 0) % 4
        new = lax.broadcasted_iota(jnp.int32, sn.shape, 1)
        sn = jnp.where(low & (new // 4 == r) & (new % 4 <= step), sn, NEG)
        m = jnp.maximum(rowmax(sc), rowmax(sn))
        ec, en = jnp.exp(sc - m), jnp.exp(sn - m)
        pc[r, 0] = dot(ec.astype(BF16), cv[r, 0]) + dot(en.astype(BF16), dkv[1])
        pc[r, 1] = jnp.broadcast_to(m, (32, HD))
        pc[r, 2] = jnp.broadcast_to(rowsum(ec) + rowsum(en), (32, HD))

    def decode_passage(r):
        q = new_q(r)
        pkv = kvall[asg_ref[r]]
        sp = dot_t(q, pkv[0]) * scale
        o1, m1, l1 = pc[r, 0], pc[r, 1], pc[r, 2]
        m = jnp.maximum(m1, rowmax(sp))
        ep = jnp.exp(sp - m[:, :1])
        a1 = jnp.exp(m1 - m)
        o = a1 * o1 + dot(ep.astype(BF16), pkv[1])
        l = a1 * l1 + rowsum(ep)
        for half in range(2):
            t = slice(half * 16, half * 16 + 16)
            pk[half, 0, r * 16 : r * 16 + 16] = o[t]
            pk[half, 1, r * 16 : r * 16 + 16] = m[t]
            pk[half, 2, r * 16 : r * 16 + 16] = l[t]

    for r in range(4):
        decode_cache(r)

    second = lax.rem(s, 2) == 1
    recv("swapk", kvprev.at[0])
    recv("swapv", kvprev.at[1])
    for i in range(4):
        m1, l1, o1 = held[i]
        q = qb[:, i * HD : (i + 1) * HD]
        s0 = jnp.where(second, dot_t(q, kvprev[0]) * scale, NEG)
        m = jnp.maximum(m1, rowmax(s0))
        a1 = jnp.exp(m1 - m)
        e0 = jnp.exp(s0 - m)
        l = a1 * l1 + rowsum(e0)
        o = (a1 * o1 + dot(e0.astype(BF16), kvprev[1])) / l
        ctx[c, :, i * HD : (i + 1) * HD] = o.astype(BF16)
        ref = ctx.at[c, :, pl.ds(i * HD, HD)]
        send(("ctx", i), ref, ref, CN)

    @pl.when(mine_parity)
    def _():
        gather_wait(mate_slot)
        for d in range(5, 8):
            gather_copy(d).start()

    far = 1 - yl
    FLOW = (1, 3, 1, 3) * 2

    def width(ci):
        return WA if ci < 4 else WB

    def columns(ci):
        at = ci * WA if ci < 4 else 4 * WA + (ci - 4) * WB
        return slice(at, at + width(ci))

    def along(f):
        return (XP, XM) if f == 1 else (XM, XP)

    def x_block(ci, d):
        at = lax.rem(x + d, 4)
        if ci < 4:
            return parta.at[ci, yl, at]
        return partb.at[ci - 4, :, at]

    def x_land(ci, k):
        return rax.at[ci, k] if ci < 4 else rbx.at[ci - 4, k]

    def x_first(ci):
        send(("m1", ci), x_block(ci, 2), x_land(ci, 0), along(FLOW[ci])[0])

    def x_second(ci):
        f = FLOW[ci]
        send(("m2", ci), x_block(ci, 4 - f), x_land(ci, 1), along(f)[1])

    def x_pass(ci):
        f = FLOW[ci]
        recv(("m1", ci), x_land(ci, 0))
        block = x_block(ci, f)
        block[...] = (block[...].astype(F32) + x_land(ci, 0)[...].astype(F32)).astype(BF16)
        send(("m3", ci), block, x_land(ci, 2), along(f)[0])

    def x_end(ci):
        recv(("m2", ci), x_land(ci, 1))
        recv(("m3", ci), x_land(ci, 2))
        return (
            x_block(ci, 0)[...].astype(F32)
            + x_land(ci, 1)[...].astype(F32)
            + x_land(ci, 2)[...].astype(F32)
        )

    def y_first(ci):
        recv(("ry", ci), ray.at[ci])
        parta[ci, yl] = (parta[ci, yl].astype(F32) + ray[ci].astype(F32)).astype(BF16)
        x_first(ci)
        x_second(ci)

    def y_last(ci):
        land = rbx.at[ci - 4, 1]
        land[...] = x_end(ci).astype(BF16)
        send(("ry", ci), land.at[far], rby.at[ci - 4], YN)

    def finish(ci):
        if ci < 4:
            total, keep, theirs = x_end(ci), fina.at[ci], finra.at[ci]
        else:
            recv(("ry", ci), rby.at[ci - 4])
            total = rbx[ci - 4, 1, yl].astype(F32) + rby[ci - 4].astype(F32)
            keep, theirs = finb.at[ci - 4], finrb.at[ci - 4]
        keep[...] = total.astype(BF16)
        send(("fin", ci), keep.at[pl.ds(pl.multiple_of(other * 16, 16), 16)], theirs, CN)

    def out_own(ci):
        return dot(ctx[c], wo[c, :, columns(ci)])

    def out_rest(ci, total):
        total = (total + dot(ctx[other], wo[other, :, columns(ci)])).astype(BF16)
        if ci < 4:
            parta[ci] = total.reshape(2, 4, 32, WA)
            send(("ry", ci), parta.at[ci, far], ray.at[ci], YN)
        else:
            partb[ci - 4] = total.reshape(2, 4, 32, WB)
            x_first(ci)

    l_wo.wait()
    begun = out_own(0)
    for i in range(WO_PIECES):
        recv(("wo", i), wo.at[other, pl.ds(i * wo_rows, wo_rows), :])
    for i in range(4):
        recv(("ctx", i), ctx.at[other, :, pl.ds(i * HD, HD)])
    out_rest(0, begun)
    for ci in (4, 5):
        out_rest(ci, out_own(ci))
    x_second(4)
    x_second(5)
    for ci in (1, 6, 7):
        out_rest(ci, out_own(ci))
    x_second(6)
    x_second(7)
    for ci in (2, 3):
        out_rest(ci, out_own(ci))

    for j in range(4):
        @pl.when((2 * j + c != s) & (2 * j + c != mate))
        def _():
            gather_wait(j)

    for r in range(4):
        decode_passage(r)
    send("part", pk.at[other], pko, CN)
    x_pass(4)
    x_pass(5)
    y_first(0)
    recv("part", pko)
    o1, m1, l1 = pk[c, 0], pk[c, 1], pk[c, 2]
    o2, m2, l2 = pko[0], pko[1], pko[2]
    mm = jnp.maximum(m1, m2)
    a1, a2 = jnp.exp(m1 - mm), jnp.exp(m2 - mm)
    dec_ctx = ((a1 * o1 + a2 * o2) / (a1 * l1 + a2 * l2)).astype(BF16)
    to = lax.broadcasted_iota(jnp.int32, (16, 64), 0)
    frm = lax.broadcasted_iota(jnp.int32, (16, 64), 1)
    for i in range(4):
        pick = ((to // 4) * 16 + i * 4 + to % 4 == frm).astype(BF16)
        dctx[c, :, i * HD : (i + 1) * HD] = dot(pick, dec_ctx).astype(BF16)
    send("dctx", dctx.at[c], dctx.at[c], CN)
    y_first(1)
    x_pass(6)
    x_pass(7)
    recv("dctx", dctx.at[other])
    for j in range(8):
        cols = slice(j * 512, (j + 1) * 512)
        dpart[j] = (dot(dctx[0], wo[0, :, cols]) + dot(dctx[1], wo[1, :, cols])).astype(BF16)
    for i in range(1, 8):
        dx, dy = i % 4, i // 4
        send(("dr", i), dpart.at[chip_at(dx, dy)], dr.at[i], dev(dx, dy))
    y_first(2)
    x_pass(0)
    y_first(3)
    x_pass(1)
    y_last(4)
    y_last(5)
    total = dpart[chip].astype(F32)
    for i in range(1, 8):
        recv(("dr", i), dr.at[i])
        total = total + dr[i].astype(F32)
    dfull[c, chip] = total.astype(BF16)
    for i in range(1, 8):
        dx, dy = i % 4, i // 4
        ref = dfull.at[c, chip]
        send(("db", i), ref, ref, dev(dx, dy))
    y_last(6)
    y_last(7)
    x_pass(2)
    x_pass(3)
    finish(0)
    finish(1)
    for i in range(1, 8):
        dx, dy = i % 4, i // 4
        recv(("db", i), dfull.at[c, chip_at(4 - dx, dy)])
    send("dall", dfull.at[c], dfull.at[c], CN)
    for ci in (4, 5, 6, 7, 2, 3):
        finish(ci)

    recv("dall", dfull.at[other])
    for a in range(2):
        for j in range(8):
            at = a * 4096 + j * 512
            dout[:, :, at : at + 512] = dfull[a, j].astype(F32).reshape(4, 4, 512).astype(BF16)
    base = pl.multiple_of(c * 4096, 4096)
    far_base = pl.multiple_of(other * 4096, 4096)
    mine = pl.ds(pl.multiple_of(c * 16, 16), 16)
    for ci in (0, 1, 4, 5, 6, 7, 2, 3):
        at = columns(ci).start
        if ci < 4:
            keep, theirs = fina.at[ci], finra.at[ci]
        else:
            keep, theirs = finb.at[ci - 4], finrb.at[ci - 4]
        pout[:, pl.ds(base + at, width(ci))] = keep[mine, :]
        recv(("fin", ci), theirs)
        pout[:, pl.ds(far_base + at, width(ci))] = theirs[...]

    for cp in sent:
        cp.wait_send()

    @pl.when(mine_parity)
    def _():
        for d in range(1, 8):
            gather_copy(d).wait_send()


def hand_over(p_in, d_in, p_out, d_out):
    p_out[...] = p_in[...]
    d_out[...] = d_in[...]


def local(
    passages, w_query, w_key, w_value, w_out, dec_hidden, cache_keys, cache_values, cache_lengths, assignment
):
    any_spec = pl.BlockSpec(memory_space=pl.ANY)
    smem = pl.BlockSpec(memory_space=pltpu.SMEM)
    vmem = pl.BlockSpec(memory_space=pltpu.VMEM)
    V = pltpu.VMEM
    shapes = (jax.ShapeDtypeStruct((16, 8192), BF16), jax.ShapeDtypeStruct((4, 4, 8192), BF16))
    results = pl.pallas_call(
        kernel,
        out_shape=shapes,
        in_specs=[any_spec] * 8 + [smem] * 2,
        out_specs=(vmem, vmem),
        scratch_shapes=[
            V((8, TOK, 1024), BF16),
            V((8, DEC, 1024), BF16),
            V((8192, 512), BF16),
            V((2 * HD, 8192), BF16),
            V((2, 512, 4096), BF16),
            V((4, 4, 8192), BF16),
            V((4, 1, 2048, HD), BF16),
            V((4, 1, 2048, HD), BF16),
            V((TOK, 512), F32),
            V((TOK, 2 * HD), F32),
            V((DEC, 512), F32),
            V((DEC, 2 * HD), F32),
            V((TOK, 512), BF16),
            V((DEC, 512), BF16),
            V((DEC, 512), BF16),
            V((2, TOK, HD), BF16),
            V((2, TOK, HD), BF16),
            V((4, 2, TOK, HD), BF16),
            V((2, DEC, HD), BF16),
            V((2, TOK, 512), BF16),
            V((4, 2, 4, 32, WA), BF16),
            V((4, 2, 4, 32, WB), BF16),
            V((4, 4, 32, WA), BF16),
            V((4, 3, 32, WA), BF16),
            V((4, 3, 2, 32, WB), BF16),
            V((4, 32, WB), BF16),
            V((4, 32, WA), BF16),
            V((4, 32, WB), BF16),
            V((4, 16, WA), BF16),
            V((4, 16, WB), BF16),
            V((4, 3, 32, HD), F32),
            V((2, 3, 64, HD), F32),
            V((3, 64, HD), F32),
            V((2, DEC, 512), BF16),
            V((8, DEC, 512), BF16),
            V((8, DEC, 512), BF16),
            V((2, 8, DEC, 512), BF16),
            pltpu.SemaphoreType.DMA((COUNT,)),
            pltpu.SemaphoreType.DMA((COUNT,)),
            pltpu.SemaphoreType.DMA((8,)),
            pltpu.SemaphoreType.DMA((8,)),
            pltpu.SemaphoreType.DMA((4,)),
        ],
        compiler_params=pltpu.CompilerParams(
            collective_id=0, has_side_effects=True, vmem_limit_bytes=60 * 2**20
        ),
        name="layer",
    )(
        passages, w_query, w_key.T, w_value.T, w_out, dec_hidden, cache_keys, cache_values, cache_lengths, assignment
    )
    return pl.pallas_call(
        hand_over,
        out_shape=shapes,
        in_specs=[vmem] * 2,
        out_specs=(vmem, vmem),
        name="hand_over",
    )(*results)


def solution(mesh):
    in_specs = (
        P("seq", "head"),
        P(None, "head"),
        P(None, "head"),
        P(None, "head"),
        P("head", None),
        P("seq", None, None),
        P("seq", "head", None, None),
        P("seq", "head", None, None),
        P("seq"),
        P("seq"),
    )
    out_specs = (P(("seq", "head"), None), P("seq", None, None))
    return jax.shard_map(local, mesh=mesh, in_specs=in_specs, out_specs=out_specs, check_vma=False)
```

```python
import functools
import math

import jax
import jax.numpy as jnp
from jax import lax
from jax.experimental import pallas as pl
from jax.experimental.pallas import tpu as pltpu
from jax.sharding import PartitionSpec as P

MESH = pl.DeviceIdType.MESH
F32 = jnp.float32
BF16 = jnp.bfloat16
HD = 128
TOK = 256
DEC = 16
NEG = -1e30
ROWS = ((0, 64), (64, 48), (112, 64), (176, 80))
HALF = ((0, 112), (112, 144))
WA, WB = 512, 512
WO_PIECES = 8


def message_ids():
    names = []
    for p in range(4):
        names += [("xp", p), ("xm", p), ("y", p)]
    names += [("xpf", 0), ("xpf", 2), ("xmf", 1), ("xmf", 3)]
    names += [("yf", dx, p) for dx in (1, 2, 3) for p in (0, 1)]
    names += [(n, p) for n in ("xpy", "xmy") for p in (2, 3)]
    names += [("xpfy", 2), ("xmfy", 3)]
    names += [("c", dx, dy, a) for dx in range(4) for dy in range(2) for a in range(2)]
    names += [("wo", i) for i in range(WO_PIECES)]
    names += ["wk", "wv", "dq", "swapk", "swapv"]
    names += [("ctx", i) for i in range(4)]
    names += [(n, i) for n in ("m1", "m2", "m3", "bl") for i in range(4, 8)]
    names += [("ry", i) for i in range(4)]
    names += [("ax", i, dx, q) for i in range(4) for dx in range(4) for q in range(2) if dx or q]
    names += [("by", i, q) for i in range(4, 8) for q in range(2)]
    names += ["part", "dall"]
    names += [("dr", i) for i in range(1, 8)] + [("db", i) for i in range(1, 8)]
    return {n: i for i, n in enumerate(names)}


IDS = message_ids()
COUNT = len(IDS)


def dot(a, b):
    return jnp.dot(a, b, preferred_element_type=F32)


def dot_t(a, b):
    return lax.dot_general(a, b, (((1,), (1,)), ((), ())), preferred_element_type=F32)


def rowmax(a):
    return jnp.max(a, axis=1, keepdims=True)


def rowsum(a):
    return jnp.sum(a, axis=1, keepdims=True)


def kernel(
    pas, wq_any, wk_any, wv_any, wo_any, dec_any, ck_any, cv_any, len_ref, asg_ref,
    pout, dout,
    xg, xd, wq, wkv, wo, dech, ck, cv,
    accq, acckv, accdq, accdkv, qb, dqb, dqo, kv, kvprev, kvall, dkv,
    ctx, parta, partb, ray, rax, rbx, rby, rbl,
    pc, pk, pko, qrows, dctx, dpart, dr, dfull,
    ssem, rsem, lsem, gs, gr,
):
    s = lax.axis_index("seq")
    h = lax.axis_index("head")
    c = lax.rem(h, 2)
    other = 1 - c
    chip = lax.div(h, 2)
    x = lax.rem(chip, 4)
    yl = lax.div(chip, 4)
    low = c == 0
    scale = 1.0 / math.sqrt(HD)

    def chip_at(dx, dy):
        return lax.rem(yl + dy, 2) * 4 + lax.rem(x + dx, 4)

    def dev(dx, dy, dc=0):
        return (s, chip_at(dx, dy) * 2 + lax.rem(c + dc, 2))

    XP, XM, YN, CN = dev(1, 0), dev(3, 0), dev(0, 1), dev(0, 0, 1)
    swap_dev = (s + 1 - 2 * lax.rem(s, 2), h)
    mate = lax.rem(s + 4, 8)
    sent = []

    def send(name, src, dst, to):
        m = IDS[name]
        cp = pltpu.make_async_remote_copy(
            src_ref=src, dst_ref=dst, send_sem=ssem.at[m], recv_sem=rsem.at[m],
            device_id=to, device_id_type=MESH,
        )
        cp.start()
        sent.append(cp)

    def recv(name, ref):
        m = IDS[name]
        pltpu.make_async_remote_copy(
            src_ref=ref, dst_ref=ref, send_sem=ssem.at[m], recv_sem=rsem.at[m],
            device_id=CN, device_id_type=MESH,
        ).wait_recv()

    def local(i, src, dst):
        cp = pltpu.make_async_copy(src, dst, lsem.at[i])
        cp.start()
        return cp

    def xs(dx, dy, rows, core):
        return xg.at[
            chip_at(dx, dy), pl.ds(rows[0], rows[1]), pl.ds(pl.multiple_of(core * 512, 512), 512)
        ]

    def kv_rows(i, core):
        return wkv.at[pl.ds(pl.multiple_of(i * HD + core * 64, 64), 64)]

    l_pas = local(0, pas, xs(0, 0, (0, TOK), c))
    l_dec = local(1, dec_any, dech)
    l_wk = local(3, wk_any, kv_rows(0, c))
    l_wv = local(4, wv_any, kv_rows(1, c))
    l_wq = local(2, wq_any, wq)

    barrier = pltpu.get_barrier_semaphore()
    for to in (XP, XM, YN, CN):
        pl.semaphore_signal(barrier, inc=1, device_id=to, device_id_type=MESH)
    z_first = lax.div(s, 4) * 4
    along_z = [z_first + lax.rem(s + d, 4) for d in range(4)]
    for to in along_z[1:] + [mate]:
        pl.semaphore_signal(barrier, inc=1, device_id=(to, h), device_id_type=MESH)
    pl.semaphore_wait(barrier, 8)

    def own(name, p, to):
        send((name, p), pas.at[pl.ds(*ROWS[p])], xs(0, 0, ROWS[p], c), to)

    def fwd(name, dx, dy, rows, to):
        ref = xs(dx, dy, rows, c)
        send(name, ref, ref, to)

    def got(name, dx, dy, rows):
        recv(name, xs(dx, dy, rows, c))

    def share(dx, dy, a):
        fwd(("c", dx, dy, a), dx, dy, HALF[a], CN)

    def shared(dx, dy):
        for a in range(2):
            recv(("c", dx, dy, a), xs(dx, dy, HALF[a], other))

    own("xp", 0, XP)
    own("xm", 1, XM)
    own("y", 2, YN)
    own("xp", 2, XP)
    own("xm", 3, XM)
    own("y", 3, YN)
    own("xp", 1, XP)
    own("xm", 0, XM)
    own("y", 0, YN)
    own("y", 1, YN)
    for a in range(2):
        send(("c", 0, 0, a), pas.at[pl.ds(*HALF[a])], xs(0, 0, HALF[a], c), CN)
    send("wk", wk_any, kv_rows(0, c), CN)
    send("wv", wv_any, kv_rows(1, c), CN)
    l_ck = local(6, ck_any, ck)
    l_cv = local(7, cv_any, cv)
    l_wo = local(5, wo_any.at[:, pl.ds(pl.multiple_of(c * 4096, 4096), 4096)], wo.at[c])

    wo_rows = 512 // WO_PIECES

    def push_wo(i):
        send(
            ("wo", i),
            wo_any.at[pl.ds(i * wo_rows, wo_rows), pl.ds(pl.multiple_of(other * 4096, 4096), 4096)],
            wo.at[c, pl.ds(i * wo_rows, wo_rows), :],
            CN,
        )

    l_dec.wait()
    for j in range(8):
        rows = dech[:, :, j * 1024 : (j + 1) * 1024].astype(F32).reshape(DEC, 1024)
        xd[j] = rows.astype(BF16)
    accq[...] = jnp.zeros_like(accq)
    acckv[...] = jnp.zeros_like(acckv)

    def project_kv(dx, dy):
        j = chip_at(dx, dy)
        cols = pl.ds(pl.multiple_of(j * 1024, 1024), 1024)
        acckv[...] += dot_t(xg[j], wkv[:, cols])

    def project_q(dx, dy):
        j = chip_at(dx, dy)
        rows = pl.ds(pl.multiple_of(j * 1024, 1024), 1024)
        accq[...] += dot(xg[j], wq[rows, :])

    def project(dx, dy):
        shared(dx, dy)
        project_kv(dx, dy)
        project_q(dx, dy)

    def project_new_q(j):
        q = dot(xd[j], wq[j * 1024 : (j + 1) * 1024, :])
        accdq[...] = q if j == 0 else accdq[...] + q

    def project_new_kv(j):
        k = dot_t(xd[j], wkv[:, j * 1024 : (j + 1) * 1024])
        accdkv[...] = k if j == 0 else accdkv[...] + k

    lane = lax.broadcasted_iota(jnp.int32, (16, HD), 1)

    def arrange_new():
        recv("dq", dqo)
        q_low = jnp.where(low, dqb[...].astype(F32), dqo[...].astype(F32)).astype(BF16)
        q_high = jnp.where(low, dqo[...].astype(F32), dqb[...].astype(F32)).astype(BF16)
        q_all = jnp.concatenate(
            [t[:, i * HD : (i + 1) * HD] for t in (q_low, q_high) for i in range(4)], axis=0
        )
        to = lax.broadcasted_iota(jnp.int32, (128, 128), 0)
        frm = lax.broadcasted_iota(jnp.int32, (128, 128), 1)
        source = (to // 64) * 64 + ((to % 16) // 4) * 16 + ((to % 64) // 16) * 4 + to % 4
        qrows[...] = dot((source == frm).astype(BF16), q_all).astype(BF16)
        l_ck.wait()
        l_cv.wait()

    def new_q(r):
        q_rows = qrows[...]
        return jnp.concatenate(
            [q_rows[r * 16 : r * 16 + 16], q_rows[64 + r * 16 : 80 + r * 16]], axis=0
        )

    def decode_cache(r):
        q = new_q(r)
        sc = dot_t(q, ck[r, 0]) * scale
        place = c * 2048 + lax.broadcasted_iota(jnp.int32, sc.shape, 1)
        sc = jnp.where(place < len_ref[r], sc, NEG)
        m = rowmax(sc)
        ec = jnp.exp(sc - m)
        pc[r, 0] = dot(ec.astype(BF16), cv[r, 0])
        pc[r, 1] = jnp.broadcast_to(m, (32, HD))
        pc[r, 2] = jnp.broadcast_to(rowsum(ec), (32, HD))

    def decode_passage(r):
        q = new_q(r)
        pkv = kvall[asg_ref[r]]
        sp = dot_t(q, pkv[0]) * scale
        sn = dot_t(q, dkv[0]) * scale
        step = lax.broadcasted_iota(jnp.int32, sn.shape, 0) % 4
        new = lax.broadcasted_iota(jnp.int32, sn.shape, 1)
        sn = jnp.where(low & (new // 4 == r) & (new % 4 <= step), sn, NEG)
        o1, m1, l1 = pc[r, 0], pc[r, 1], pc[r, 2]
        m = jnp.maximum(m1, jnp.maximum(rowmax(sp), rowmax(sn)))
        ep, en = jnp.exp(sp - m[:, :1]), jnp.exp(sn - m[:, :1])
        a1 = jnp.exp(m1 - m)
        o = a1 * o1 + dot(ep.astype(BF16), pkv[1]) + dot(en.astype(BF16), dkv[1])
        l = a1 * l1 + rowsum(ep) + rowsum(en)
        for half in range(2):
            t = slice(half * 16, half * 16 + 16)
            at = half * 64 + r * 16
            pk[0, at : at + 16] = o[t]
            pk[1, at : at + 16] = jnp.where(lane < 64, m[t], l[t])

    got(("xm", 1), 1, 0, ROWS[1])
    fwd(("yf", 1, 1), 1, 0, ROWS[1], YN)
    fwd(("xmf", 1), 1, 0, ROWS[1], XM)
    got(("y", 2), 0, 1, ROWS[2])
    fwd(("xpy", 2), 0, 1, ROWS[2], XP)
    got(("xp", 0), 3, 0, ROWS[0])
    fwd(("yf", 3, 0), 3, 0, ROWS[0], YN)
    fwd(("xpf", 0), 3, 0, ROWS[0], XP)
    l_wq.wait()
    for j in range(8):
        project_new_q(j)
    dqb[...] = accdq[...].astype(BF16)
    send("dq", dqb, dqo, CN)
    got(("xp", 2), 3, 0, ROWS[2])
    fwd(("xpf", 2), 3, 0, ROWS[2], XP)
    got(("y", 3), 0, 1, ROWS[3])
    fwd(("xmy", 3), 0, 1, ROWS[3], XM)
    fwd(("xpy", 3), 0, 1, ROWS[3], XP)
    got(("xm", 3), 1, 0, ROWS[3])
    fwd(("xmf", 3), 1, 0, ROWS[3], XM)
    fwd(("xmy", 2), 0, 1, ROWS[2], XM)
    own("xp", 3, XP)
    own("xm", 2, XM)
    share(0, 1, 1)
    arrange_new()
    decode_cache(0)
    got(("xp", 1), 3, 0, ROWS[1])
    fwd(("yf", 3, 1), 3, 0, ROWS[1], YN)
    share(3, 0, 0)
    got(("xm", 0), 1, 0, ROWS[0])
    fwd(("yf", 1, 0), 1, 0, ROWS[0], YN)
    share(1, 0, 0)
    decode_cache(1)
    l_wk.wait()
    l_wv.wait()
    l_pas.wait()
    recv("wk", kv_rows(0, other))
    recv("wv", kv_rows(1, other))
    push_wo(0)
    got(("xpy", 2), 3, 1, ROWS[2])
    fwd(("xpfy", 2), 3, 1, ROWS[2], XP)
    got(("xmf", 1), 2, 0, ROWS[1])
    fwd(("yf", 2, 1), 2, 0, ROWS[1], YN)
    decode_cache(2)
    got(("xpf", 0), 2, 0, ROWS[0])
    fwd(("yf", 2, 0), 2, 0, ROWS[0], YN)
    share(2, 0, 0)
    push_wo(1)
    decode_cache(3)
    got(("xmy", 3), 1, 1, ROWS[3])
    fwd(("xmfy", 3), 1, 1, ROWS[3], XM)
    got(("y", 0), 0, 1, ROWS[0])
    got(("y", 1), 0, 1, ROWS[1])
    share(0, 1, 0)
    for j in range(8):
        project_new_kv(j)
    for i in range(2):
        dkv[i] = accdkv[:, i * HD : (i + 1) * HD].astype(BF16)
    project(0, 0)
    got(("xpf", 2), 2, 0, ROWS[2])
    got(("xmf", 3), 2, 0, ROWS[3])
    share(2, 0, 1)
    push_wo(2)
    project(0, 1)
    got(("yf", 3, 0), 3, 1, ROWS[0])
    got(("yf", 1, 1), 1, 1, ROWS[1])
    got(("yf", 3, 1), 3, 1, ROWS[1])
    got(("yf", 1, 0), 1, 1, ROWS[0])
    share(3, 1, 0)
    share(1, 1, 0)
    got(("xpy", 3), 3, 1, ROWS[3])
    share(3, 1, 1)
    project(2, 0)
    got(("xmy", 2), 1, 1, ROWS[2])
    share(1, 1, 1)
    got(("xp", 3), 3, 0, ROWS[3])
    share(3, 0, 1)
    got(("xm", 2), 1, 0, ROWS[2])
    share(1, 0, 1)
    project(3, 1)
    got(("xpfy", 2), 2, 1, ROWS[2])
    got(("xmfy", 3), 2, 1, ROWS[3])
    share(2, 1, 1)
    got(("yf", 2, 1), 2, 1, ROWS[1])
    got(("yf", 2, 0), 2, 1, ROWS[0])
    share(2, 1, 0)
    project(1, 1)
    last = ((3, 0), (1, 0), (2, 1))
    for place in last:
        shared(*place)
        project_kv(*place)

    for i in range(2):
        kv[i] = acckv[:, i * HD : (i + 1) * HD].astype(BF16)
    send("swapk", kv.at[0], kvprev.at[0], swap_dev)
    send("swapv", kv.at[1], kvprev.at[1], swap_dev)
    for i in range(3, WO_PIECES):
        push_wo(i)
    for place in last:
        project_q(*place)
    qb[...] = accq[...].astype(BF16)

    mine_parity = lax.rem(s, 2) == c
    slot = lax.div(s, 2)
    mate_slot = lax.div(mate, 2)

    def gather_copy(d):
        to = mate if d == 4 else along_z[d % 4]
        if d < 5:
            src, at = kv, slot
        else:
            src, at = kvall.at[mate_slot], mate_slot
        return pltpu.make_async_remote_copy(
            src_ref=src, dst_ref=kvall.at[at], send_sem=gs.at[d], recv_sem=gr.at[at],
            device_id=(to, h), device_id_type=MESH,
        )

    def gather_wait(j):
        pltpu.make_async_remote_copy(
            src_ref=kv, dst_ref=kvall.at[j], send_sem=gs.at[0], recv_sem=gr.at[j],
            device_id=CN, device_id_type=MESH,
        ).wait_recv()

    @pl.when(mine_parity)
    def _():
        gather_copy(4).start()
        for d in range(1, 4):
            gather_copy(d).start()
        kvall[slot] = kv[...]

    row = lax.broadcasted_iota(jnp.int32, (TOK, TOK), 0)
    col = lax.broadcasted_iota(jnp.int32, (TOK, TOK), 1)
    held = []
    for i in range(4):
        q = qb[:, i * HD : (i + 1) * HD]
        s1 = jnp.where(row >= col, dot_t(q, kv[0]) * scale, NEG)
        m1 = rowmax(s1)
        e1 = jnp.exp(s1 - m1)
        held.append((m1, rowsum(e1), dot(e1.astype(BF16), kv[1])))

    @pl.when(mine_parity)
    def _():
        gather_wait(mate_slot)
        for d in range(5, 8):
            gather_copy(d).start()

    second = lax.rem(s, 2) == 1
    recv("swapk", kvprev.at[0])
    scored = []
    for i in range(4):
        m1, l1, o1 = held[i]
        q = qb[:, i * HD : (i + 1) * HD]
        s0 = jnp.where(second, dot_t(q, kvprev[0]) * scale, NEG)
        m = jnp.maximum(m1, rowmax(s0))
        a1 = jnp.exp(m1 - m)
        e0 = jnp.exp(s0 - m)
        inv = 1.0 / (a1 * l1 + rowsum(e0))
        scored.append((e0.astype(BF16), a1 * o1, inv))
    recv("swapv", kvprev.at[1])
    for i in range(4):
        e0, o1, inv = scored[i]
        o = (o1 + dot(e0, kvprev[1])) * inv
        ctx[c, :, i * HD : (i + 1) * HD] = o.astype(BF16)
        ref = ctx.at[c, :, pl.ds(i * HD, HD)]
        send(("ctx", i), ref, ref, CN)

    far = 1 - yl
    FLOW = (1, 3, 1, 3) * 2
    base = pl.multiple_of(c * 4096, 4096)
    far_base = pl.multiple_of(other * 4096, 4096)

    def width(ci):
        return WA if ci < 4 else WB

    def columns(ci):
        at = ci * WA if ci < 4 else 4 * WA + (ci - 4) * WB
        return slice(at, at + width(ci))

    def rows_of(core):
        return pl.ds(pl.multiple_of(core * 16, 16), 16)

    def along(f):
        return (XP, XM) if f == 1 else (XM, XP)

    def y_first(ci):
        recv(("ry", ci), ray.at[ci])
        parta[ci, yl] = (parta[ci, yl].astype(F32) + ray[ci].astype(F32)).astype(BF16)
        for dx in (2, 1, 3, 0):
            for q in range(2):
                if dx or q:
                    src = parta.at[ci, yl, lax.rem(x + dx, 4), rows_of(lax.rem(c + q, 2))]
                    send(("ax", ci, dx, q), src, rax.at[ci, c, dx], dev(dx, 0, q))

    def x_block(ci, d):
        return partb.at[ci - 4, :, lax.rem(x + d, 4)]

    def x_land(ci, k):
        return rbx.at[ci - 4, k]

    def x_first(ci):
        send(("m1", ci), x_block(ci, 2), x_land(ci, 0), along(FLOW[ci])[0])

    def x_second(ci):
        f = FLOW[ci]
        send(("m2", ci), x_block(ci, 4 - f), x_land(ci, 1), along(f)[1])

    def x_pass(ci):
        f = FLOW[ci]
        recv(("m1", ci), x_land(ci, 0))
        block = x_block(ci, f)
        block[...] = (block[...].astype(F32) + x_land(ci, 0)[...].astype(F32)).astype(BF16)
        send(("m3", ci), block, x_land(ci, 2), along(f)[0])

    def y_last(ci):
        recv(("m2", ci), x_land(ci, 1))
        recv(("m3", ci), x_land(ci, 2))
        land = x_land(ci, 1)
        land[...] = (
            x_block(ci, 0)[...].astype(F32) + land[...].astype(F32) + x_land(ci, 2)[...].astype(F32)
        ).astype(BF16)
        for q in range(2):
            src = land.at[far, rows_of(lax.rem(c + q, 2))]
            send(("by", ci, q), src, rby.at[ci - 4, c], dev(0, 1, q))
        send(("bl", ci), land.at[yl, rows_of(other)], rbl.at[ci - 4], CN)

    def finish(ci):
        at = columns(ci).start
        if ci < 4:
            for dx in range(4):
                for q in range(2):
                    if dx or q:
                        recv(("ax", ci, dx, q), rax.at[ci, lax.rem(c + q, 2), dx])
            near = parta[ci, yl, x, rows_of(c)].astype(F32)
            for dx in range(1, 4):
                near += rax[ci, c, dx].astype(F32)
            away = rax[ci, other, 0].astype(F32)
            for dx in range(1, 4):
                away += rax[ci, other, dx].astype(F32)
        else:
            for q in range(2):
                recv(("by", ci, q), rby.at[ci - 4, lax.rem(c + q, 2)])
            recv(("bl", ci), rbl.at[ci - 4])
            near = rbx[ci - 4, 1, yl, rows_of(c)].astype(F32) + rby[ci - 4, c].astype(F32)
            away = rbl[ci - 4].astype(F32) + rby[ci - 4, other].astype(F32)
        pout[:, pl.ds(base + at, width(ci))] = near.astype(BF16)
        pout[:, pl.ds(far_base + at, width(ci))] = away.astype(BF16)

    def out_own(ci):
        return dot(ctx[c], wo[c, :, columns(ci)])

    def out_rest(ci, total):
        total = (total + dot(ctx[other], wo[other, :, columns(ci)])).astype(BF16)
        if ci < 4:
            parta[ci] = total.reshape(2, 4, 32, WA)
            send(("ry", ci), parta.at[ci, far], ray.at[ci], YN)
        else:
            partb[ci - 4] = total.reshape(2, 4, 32, WB)
            x_first(ci)

    l_wo.wait()
    begun = out_own(7)
    begun_b = out_own(0)
    for i in range(WO_PIECES):
        recv(("wo", i), wo.at[other, pl.ds(i * wo_rows, wo_rows), :])
    for i in range(4):
        recv(("ctx", i), ctx.at[other, :, pl.ds(i * HD, HD)])
    out_rest(7, begun)
    x_second(7)
    out_rest(0, begun_b)
    out_rest(6, out_own(6))
    x_second(6)
    out_rest(2, out_own(2))
    out_rest(5, out_own(5))
    x_second(5)
    out_rest(4, out_own(4))
    x_pass(7)
    for j in range(4):
        @pl.when((2 * j + c != s) & (2 * j + c != mate))
        def _():
            gather_wait(j)

    for r in range(4):
        decode_passage(r)
    send("part", pk, pko, CN)
    x_pass(6)
    x_second(4)
    out_rest(1, out_own(1))
    y_first(0)
    recv("part", pko)
    o1, m1, l1 = pk[0], pk[1, :, 0:1], pk[1, :, 64:65]
    o2, m2, l2 = pko[0], pko[1, :, 0:1], pko[1, :, 64:65]
    mm = jnp.maximum(m1, m2)
    a1, a2 = jnp.exp(m1 - mm), jnp.exp(m2 - mm)
    dec_ctx = ((a1 * o1 + a2 * o2) / (a1 * l1 + a2 * l2)).astype(BF16)
    to = lax.broadcasted_iota(jnp.int32, (16, 64), 0)
    frm = lax.broadcasted_iota(jnp.int32, (16, 64), 1)
    for i in range(4):
        pick = ((to // 4) * 16 + i * 4 + to % 4 == frm).astype(BF16)
        for half in range(2):
            chosen = dot(pick, dec_ctx[half * 64 : half * 64 + 64])
            dctx[half, :, i * HD : (i + 1) * HD] = chosen.astype(BF16)
    for j in range(8):
        cols = slice(j * 512, (j + 1) * 512)
        dpart[j] = (dot(dctx[0], wo[0, :, cols]) + dot(dctx[1], wo[1, :, cols])).astype(BF16)
    for i in (6, 2, 5, 7, 1, 3, 4):
        dx, dy = i % 4, i // 4
        send(("dr", i), dpart.at[chip_at(dx, dy)], dr.at[i], dev(dx, dy))
    y_first(2)
    out_rest(3, out_own(3))
    x_pass(5)
    x_pass(4)
    y_last(6)
    y_first(1)
    total = dpart[chip].astype(F32)
    for i in range(1, 8):
        recv(("dr", i), dr.at[i])
        total = total + dr[i].astype(F32)
    dfull[c, chip] = total.astype(BF16)
    for i in (6, 2, 5, 7, 1, 3, 4):
        dx, dy = i % 4, i // 4
        ref = dfull.at[c, chip]
        send(("db", i), ref, ref, dev(dx, dy))
    y_last(7)
    y_last(4)
    y_first(3)
    finish(0)
    y_last(5)
    for i in range(1, 8):
        dx, dy = i % 4, i // 4
        recv(("db", i), dfull.at[c, chip_at(4 - dx, dy)])
    send("dall", dfull.at[c], dfull.at[c], CN)
    finish(6)
    finish(2)
    finish(1)
    finish(7)
    finish(4)
    finish(3)
    finish(5)

    recv("dall", dfull.at[other])
    for a in range(2):
        for j in range(8):
            at = a * 4096 + j * 512
            dout[:, :, at : at + 512] = dfull[a, j].astype(F32).reshape(4, 4, 512).astype(BF16)

    for cp in sent:
        cp.wait_send()

    @pl.when(mine_parity)
    def _():
        for d in range(1, 8):
            gather_copy(d).wait_send()


def hand_over(p_in, d_in, p_out, d_out):
    p_out[...] = p_in[...]
    d_out[...] = d_in[...]


def local(
    passages, w_query, w_key, w_value, w_out, dec_hidden, cache_keys, cache_values, cache_lengths, assignment
):
    any_spec = pl.BlockSpec(memory_space=pl.ANY)
    smem = pl.BlockSpec(memory_space=pltpu.SMEM)
    vmem = pl.BlockSpec(memory_space=pltpu.VMEM)
    V = pltpu.VMEM
    shapes = (jax.ShapeDtypeStruct((16, 8192), BF16), jax.ShapeDtypeStruct((4, 4, 8192), BF16))
    results = pl.pallas_call(
        kernel,
        out_shape=shapes,
        in_specs=[any_spec] * 8 + [smem] * 2,
        out_specs=(vmem, vmem),
        scratch_shapes=[
            V((8, TOK, 1024), BF16),
            V((8, DEC, 1024), BF16),
            V((8192, 512), BF16),
            V((2 * HD, 8192), BF16),
            V((2, 512, 4096), BF16),
            V((4, 4, 8192), BF16),
            V((4, 1, 2048, HD), BF16),
            V((4, 1, 2048, HD), BF16),
            V((TOK, 512), F32),
            V((TOK, 2 * HD), F32),
            V((DEC, 512), F32),
            V((DEC, 2 * HD), F32),
            V((TOK, 512), BF16),
            V((DEC, 512), BF16),
            V((DEC, 512), BF16),
            V((2, TOK, HD), BF16),
            V((2, TOK, HD), BF16),
            V((4, 2, TOK, HD), BF16),
            V((2, DEC, HD), BF16),
            V((2, TOK, 512), BF16),
            V((4, 2, 4, 32, WA), BF16),
            V((4, 2, 4, 32, WB), BF16),
            V((4, 4, 32, WA), BF16),
            V((4, 2, 4, 16, WA), BF16),
            V((4, 3, 2, 32, WB), BF16),
            V((4, 2, 16, WB), BF16),
            V((4, 16, WB), BF16),
            V((4, 3, 32, HD), F32),
            V((2, 128, HD), F32),
            V((2, 128, HD), F32),
            V((128, HD), BF16),
            V((2, DEC, 512), BF16),
            V((8, DEC, 512), BF16),
            V((8, DEC, 512), BF16),
            V((2, 8, DEC, 512), BF16),
            pltpu.SemaphoreType.DMA((COUNT,)),
            pltpu.SemaphoreType.DMA((COUNT,)),
            pltpu.SemaphoreType.DMA((8,)),
            pltpu.SemaphoreType.DMA((8,)),
            pltpu.SemaphoreType.DMA((4,)),
        ],
        compiler_params=pltpu.CompilerParams(
            collective_id=0, has_side_effects=True, vmem_limit_bytes=60 * 2**20
        ),
        name="layer",
    )(
        passages, w_query, w_key.T, w_value.T, w_out, dec_hidden, cache_keys, cache_values, cache_lengths, assignment
    )
    return pl.pallas_call(
        hand_over,
        out_shape=shapes,
        in_specs=[vmem] * 2,
        out_specs=(vmem, vmem),
        name="hand_over",
    )(*results)


def solution(mesh):
    in_specs = (
        P("seq", "head"),
        P(None, "head"),
        P(None, "head"),
        P(None, "head"),
        P("head", None),
        P("seq", None, None),
        P("seq", "head", None, None),
        P("seq", "head", None, None),
        P("seq"),
        P("seq"),
    )
    out_specs = (P(("seq", "head"), None), P("seq", None, None))
    return jax.shard_map(local, mesh=mesh, in_specs=in_specs, out_specs=out_specs, check_vma=False)
```

```python
import functools
import math

import jax
import jax.numpy as jnp
from jax import lax
from jax.experimental import pallas as pl
from jax.experimental.pallas import tpu as pltpu
from jax.sharding import PartitionSpec as P

MESH = pl.DeviceIdType.MESH
F32 = jnp.float32
BF16 = jnp.bfloat16
HD = 128
TOK = 256
DEC = 16
NEG = -1e30
ROWS = ((0, 64), (64, 48), (112, 64), (176, 80))
HALF = ((0, 112), (112, 144))
WA, WB = 512, 512
WO_PIECES = 8


def message_ids():
    names = []
    for p in range(4):
        names += [("xp", p), ("xm", p), ("y", p)]
    names += [("xpf", 0), ("xpf", 2), ("xmf", 1), ("xmf", 3)]
    names += [("yf", dx, p) for dx in (1, 2, 3) for p in (0, 1)]
    names += [(n, p) for n in ("xpy", "xmy") for p in (2, 3)]
    names += [("xpfy", 2), ("xmfy", 3)]
    names += [("c", dx, dy, a) for dx in range(4) for dy in range(2) for a in range(2)]
    names += [("wo", i) for i in range(WO_PIECES)]
    names += ["wk", "wv", "dq", "swapk", "swapv"]
    names += [("ctx", i) for i in range(4)]
    names += [(n, i) for n in ("m1", "m2", "m3", "bl") for i in range(4, 8)]
    names += [("ry", i) for i in range(4)]
    names += [("ax", i, dx, q) for i in range(4) for dx in range(4) for q in range(2) if dx or q]
    names += [("by", i, q) for i in range(4, 8) for q in range(2)]
    names += ["part", "dall"]
    names += [("dr", i) for i in range(1, 8)] + [("db", i) for i in range(1, 8)]
    return {n: i for i, n in enumerate(names)}


IDS = message_ids()
COUNT = len(IDS)


def dot(a, b):
    return jnp.dot(a, b, preferred_element_type=F32)


def dot_t(a, b):
    return lax.dot_general(a, b, (((1,), (1,)), ((), ())), preferred_element_type=F32)


def rowmax(a):
    return jnp.max(a, axis=1, keepdims=True)


def rowsum(a):
    return jnp.sum(a, axis=1, keepdims=True)


def kernel(
    pas, wq_any, wk_any, wv_any, wo_any, dec_any, ck_any, cv_any, len_ref, asg_ref,
    pout, dout,
    xg, xd, wq, wkv, wo, dech, ck, cv,
    accq, acckv, accdq, accdkv, qb, dqb, dqo, kv, kvprev, kvall, dkv,
    ctx, parta, partb, ray, rax, rbx, rby, rbl,
    pc, pk, pko, qrows, dctx, dpart, dr, dfull,
    ssem, rsem, lsem, gs, gr,
):
    s = lax.axis_index("seq")
    h = lax.axis_index("head")
    c = lax.rem(h, 2)
    other = 1 - c
    chip = lax.div(h, 2)
    x = lax.rem(chip, 4)
    yl = lax.div(chip, 4)
    low = c == 0
    scale = 1.0 / math.sqrt(HD)

    def chip_at(dx, dy):
        return lax.rem(yl + dy, 2) * 4 + lax.rem(x + dx, 4)

    def dev(dx, dy, dc=0):
        return (s, chip_at(dx, dy) * 2 + lax.rem(c + dc, 2))

    XP, XM, YN, CN = dev(1, 0), dev(3, 0), dev(0, 1), dev(0, 0, 1)
    swap_dev = (s + 1 - 2 * lax.rem(s, 2), h)
    mate = lax.rem(s + 4, 8)
    sent = []

    def send(name, src, dst, to):
        m = IDS[name]
        cp = pltpu.make_async_remote_copy(
            src_ref=src, dst_ref=dst, send_sem=ssem.at[m], recv_sem=rsem.at[m],
            device_id=to, device_id_type=MESH,
        )
        cp.start()
        sent.append(cp)

    def recv(name, ref):
        m = IDS[name]
        pltpu.make_async_remote_copy(
            src_ref=ref, dst_ref=ref, send_sem=ssem.at[m], recv_sem=rsem.at[m],
            device_id=CN, device_id_type=MESH,
        ).wait_recv()

    def local(i, src, dst):
        cp = pltpu.make_async_copy(src, dst, lsem.at[i])
        cp.start()
        return cp

    def xs(dx, dy, rows, core):
        return xg.at[
            chip_at(dx, dy), pl.ds(rows[0], rows[1]), pl.ds(pl.multiple_of(core * 512, 512), 512)
        ]

    def kv_rows(i, core):
        return wkv.at[pl.ds(pl.multiple_of(i * HD + core * 64, 64), 64)]

    l_pas = local(0, pas, xs(0, 0, (0, TOK), c))
    l_dec = local(1, dec_any, dech)
    l_wk = local(3, wk_any, kv_rows(0, c))
    l_wv = local(4, wv_any, kv_rows(1, c))
    l_wq = local(2, wq_any, wq)

    barrier = pltpu.get_barrier_semaphore()
    for to in (XP, XM, YN, CN):
        pl.semaphore_signal(barrier, inc=1, device_id=to, device_id_type=MESH)
    z_first = lax.div(s, 4) * 4
    along_z = [z_first + lax.rem(s + d, 4) for d in range(4)]
    for to in along_z[1:] + [mate]:
        pl.semaphore_signal(barrier, inc=1, device_id=(to, h), device_id_type=MESH)
    pl.semaphore_wait(barrier, 8)

    def own(name, p, to):
        send((name, p), pas.at[pl.ds(*ROWS[p])], xs(0, 0, ROWS[p], c), to)

    def fwd(name, dx, dy, rows, to):
        ref = xs(dx, dy, rows, c)
        send(name, ref, ref, to)

    def got(name, dx, dy, rows):
        recv(name, xs(dx, dy, rows, c))

    def share(dx, dy, a):
        fwd(("c", dx, dy, a), dx, dy, HALF[a], CN)

    def shared(dx, dy):
        for a in range(2):
            recv(("c", dx, dy, a), xs(dx, dy, HALF[a], other))

    own("xp", 0, XP)
    own("xm", 1, XM)
    own("y", 2, YN)
    own("xp", 2, XP)
    own("xm", 3, XM)
    own("y", 3, YN)
    own("xp", 1, XP)
    own("xm", 0, XM)
    own("y", 0, YN)
    own("y", 1, YN)
    for a in range(2):
        send(("c", 0, 0, a), pas.at[pl.ds(*HALF[a])], xs(0, 0, HALF[a], c), CN)
    send("wk", wk_any, kv_rows(0, c), CN)
    send("wv", wv_any, kv_rows(1, c), CN)
    l_ck = local(6, ck_any, ck)
    l_cv = local(7, cv_any, cv)
    l_wo = local(5, wo_any.at[:, pl.ds(pl.multiple_of(c * 4096, 4096), 4096)], wo.at[c])

    wo_rows = 512 // WO_PIECES

    def push_wo(i):
        send(
            ("wo", i),
            wo_any.at[pl.ds(i * wo_rows, wo_rows), pl.ds(pl.multiple_of(other * 4096, 4096), 4096)],
            wo.at[c, pl.ds(i * wo_rows, wo_rows), :],
            CN,
        )

    l_dec.wait()
    for j in range(8):
        rows = dech[:, :, j * 1024 : (j + 1) * 1024].astype(F32).reshape(DEC, 1024)
        xd[j] = rows.astype(BF16)
    accq[...] = jnp.zeros_like(accq)
    acckv[...] = jnp.zeros_like(acckv)

    def project_kv(dx, dy):
        j = chip_at(dx, dy)
        cols = pl.ds(pl.multiple_of(j * 1024, 1024), 1024)
        acckv[...] += dot_t(xg[j], wkv[:, cols])

    def project_q(dx, dy):
        j = chip_at(dx, dy)
        rows = pl.ds(pl.multiple_of(j * 1024, 1024), 1024)
        accq[...] += dot(xg[j], wq[rows, :])

    def project(dx, dy):
        shared(dx, dy)
        project_kv(dx, dy)
        project_q(dx, dy)

    def project_new_q(j):
        q = dot(xd[j], wq[j * 1024 : (j + 1) * 1024, :])
        accdq[...] = q if j == 0 else accdq[...] + q

    def project_new_kv(j):
        k = dot_t(xd[j], wkv[:, j * 1024 : (j + 1) * 1024])
        accdkv[...] = k if j == 0 else accdkv[...] + k

    lane = lax.broadcasted_iota(jnp.int32, (16, HD), 1)

    def arrange_new():
        recv("dq", dqo)
        q_low = jnp.where(low, dqb[...].astype(F32), dqo[...].astype(F32)).astype(BF16)
        q_high = jnp.where(low, dqo[...].astype(F32), dqb[...].astype(F32)).astype(BF16)
        q_all = jnp.concatenate(
            [t[:, i * HD : (i + 1) * HD] for t in (q_low, q_high) for i in range(4)], axis=0
        )
        to = lax.broadcasted_iota(jnp.int32, (128, 128), 0)
        frm = lax.broadcasted_iota(jnp.int32, (128, 128), 1)
        source = (to // 64) * 64 + ((to % 16) // 4) * 16 + ((to % 64) // 16) * 4 + to % 4
        qrows[...] = dot((source == frm).astype(BF16), q_all).astype(BF16)
        l_ck.wait()
        l_cv.wait()

    def new_q(r):
        q_rows = qrows[...]
        return jnp.concatenate(
            [q_rows[r * 16 : r * 16 + 16], q_rows[64 + r * 16 : 80 + r * 16]], axis=0
        )

    def decode_cache(r):
        q = new_q(r)
        sc = dot_t(q, ck[r, 0]) * scale
        place = c * 2048 + lax.broadcasted_iota(jnp.int32, sc.shape, 1)
        sc = jnp.where(place < len_ref[r], sc, NEG)
        m = rowmax(sc)
        ec = jnp.exp(sc - m)
        pc[r, 0] = dot(ec.astype(BF16), cv[r, 0])
        pc[r, 1] = jnp.broadcast_to(m, (32, HD))
        pc[r, 2] = jnp.broadcast_to(rowsum(ec), (32, HD))

    def decode_passage(r):
        q = new_q(r)
        pkv = kvall[asg_ref[r]]
        sp = dot_t(q, pkv[0]) * scale
        sn = dot_t(q, dkv[0]) * scale
        step = lax.broadcasted_iota(jnp.int32, sn.shape, 0) % 4
        new = lax.broadcasted_iota(jnp.int32, sn.shape, 1)
        sn = jnp.where(low & (new // 4 == r) & (new % 4 <= step), sn, NEG)
        o1, m1, l1 = pc[r, 0], pc[r, 1], pc[r, 2]
        m = jnp.maximum(m1, jnp.maximum(rowmax(sp), rowmax(sn)))
        ep, en = jnp.exp(sp - m[:, :1]), jnp.exp(sn - m[:, :1])
        a1 = jnp.exp(m1 - m)
        o = a1 * o1 + dot(ep.astype(BF16), pkv[1]) + dot(en.astype(BF16), dkv[1])
        l = a1 * l1 + rowsum(ep) + rowsum(en)
        for half in range(2):
            t = slice(half * 16, half * 16 + 16)
            at = half * 64 + r * 16
            pk[0, at : at + 16] = o[t]
            pk[1, at : at + 16] = jnp.where(lane < 64, m[t], l[t])

    got(("xm", 1), 1, 0, ROWS[1])
    fwd(("yf", 1, 1), 1, 0, ROWS[1], YN)
    fwd(("xmf", 1), 1, 0, ROWS[1], XM)
    got(("y", 2), 0, 1, ROWS[2])
    fwd(("xpy", 2), 0, 1, ROWS[2], XP)
    got(("xp", 0), 3, 0, ROWS[0])
    fwd(("yf", 3, 0), 3, 0, ROWS[0], YN)
    fwd(("xpf", 0), 3, 0, ROWS[0], XP)
    l_wq.wait()
    for j in range(8):
        project_new_q(j)
    dqb[...] = accdq[...].astype(BF16)
    send("dq", dqb, dqo, CN)
    got(("xp", 2), 3, 0, ROWS[2])
    fwd(("xpf", 2), 3, 0, ROWS[2], XP)
    got(("y", 3), 0, 1, ROWS[3])
    fwd(("xmy", 3), 0, 1, ROWS[3], XM)
    fwd(("xpy", 3), 0, 1, ROWS[3], XP)
    got(("xm", 3), 1, 0, ROWS[3])
    fwd(("xmf", 3), 1, 0, ROWS[3], XM)
    fwd(("xmy", 2), 0, 1, ROWS[2], XM)
    own("xp", 3, XP)
    own("xm", 2, XM)
    share(0, 1, 1)
    arrange_new()
    decode_cache(0)
    got(("xp", 1), 3, 0, ROWS[1])
    fwd(("yf", 3, 1), 3, 0, ROWS[1], YN)
    share(3, 0, 0)
    got(("xm", 0), 1, 0, ROWS[0])
    fwd(("yf", 1, 0), 1, 0, ROWS[0], YN)
    share(1, 0, 0)
    decode_cache(1)
    l_wk.wait()
    l_wv.wait()
    l_pas.wait()
    recv("wk", kv_rows(0, other))
    recv("wv", kv_rows(1, other))
    push_wo(0)
    got(("xpy", 2), 3, 1, ROWS[2])
    fwd(("xpfy", 2), 3, 1, ROWS[2], XP)
    got(("xmf", 1), 2, 0, ROWS[1])
    fwd(("yf", 2, 1), 2, 0, ROWS[1], YN)
    decode_cache(2)
    got(("xpf", 0), 2, 0, ROWS[0])
    fwd(("yf", 2, 0), 2, 0, ROWS[0], YN)
    share(2, 0, 0)
    push_wo(1)
    decode_cache(3)
    got(("xmy", 3), 1, 1, ROWS[3])
    fwd(("xmfy", 3), 1, 1, ROWS[3], XM)
    got(("y", 0), 0, 1, ROWS[0])
    got(("y", 1), 0, 1, ROWS[1])
    share(0, 1, 0)
    for j in range(8):
        project_new_kv(j)
    for i in range(2):
        dkv[i] = accdkv[:, i * HD : (i + 1) * HD].astype(BF16)
    project(0, 0)
    got(("xpf", 2), 2, 0, ROWS[2])
    got(("xmf", 3), 2, 0, ROWS[3])
    share(2, 0, 1)
    push_wo(2)
    project(0, 1)
    got(("yf", 3, 0), 3, 1, ROWS[0])
    got(("yf", 1, 1), 1, 1, ROWS[1])
    got(("yf", 3, 1), 3, 1, ROWS[1])
    got(("yf", 1, 0), 1, 1, ROWS[0])
    share(3, 1, 0)
    share(1, 1, 0)
    got(("xpy", 3), 3, 1, ROWS[3])
    share(3, 1, 1)
    project(2, 0)
    got(("xmy", 2), 1, 1, ROWS[2])
    share(1, 1, 1)
    got(("xp", 3), 3, 0, ROWS[3])
    share(3, 0, 1)
    got(("xm", 2), 1, 0, ROWS[2])
    share(1, 0, 1)
    project(3, 1)
    got(("xpfy", 2), 2, 1, ROWS[2])
    got(("xmfy", 3), 2, 1, ROWS[3])
    share(2, 1, 1)
    got(("yf", 2, 1), 2, 1, ROWS[1])
    got(("yf", 2, 0), 2, 1, ROWS[0])
    share(2, 1, 0)
    project(1, 1)
    last = ((3, 0), (1, 0), (2, 1))
    for place in last:
        shared(*place)
        project_kv(*place)

    for i in range(2):
        kv[i] = acckv[:, i * HD : (i + 1) * HD].astype(BF16)
    send("swapk", kv.at[0], kvprev.at[0], swap_dev)
    send("swapv", kv.at[1], kvprev.at[1], swap_dev)
    mine_parity = lax.rem(s, 2) == c
    slot = lax.div(s, 2)
    mate_slot = lax.div(mate, 2)

    def gather_copy(d):
        to = mate if d == 4 else along_z[d % 4]
        if d < 5:
            src, at = kv, slot
        else:
            src, at = kvall.at[mate_slot], mate_slot
        return pltpu.make_async_remote_copy(
            src_ref=src, dst_ref=kvall.at[at], send_sem=gs.at[d], recv_sem=gr.at[at],
            device_id=(to, h), device_id_type=MESH,
        )

    def gather_wait(j):
        pltpu.make_async_remote_copy(
            src_ref=kv, dst_ref=kvall.at[j], send_sem=gs.at[0], recv_sem=gr.at[j],
            device_id=CN, device_id_type=MESH,
        ).wait_recv()

    @pl.when(mine_parity)
    def _():
        gather_copy(4).start()
        for d in range(1, 4):
            gather_copy(d).start()
        kvall[slot] = kv[...]

    for i in range(3, WO_PIECES):
        push_wo(i)
    for place in last:
        project_q(*place)
    qb[...] = accq[...].astype(BF16)

    row = lax.broadcasted_iota(jnp.int32, (TOK, TOK), 0)
    col = lax.broadcasted_iota(jnp.int32, (TOK, TOK), 1)
    held = []
    for i in range(4):
        q = qb[:, i * HD : (i + 1) * HD]
        s1 = jnp.where(row >= col, dot_t(q, kv[0]) * scale, NEG)
        m1 = rowmax(s1)
        e1 = jnp.exp(s1 - m1)
        held.append((m1, rowsum(e1), dot(e1.astype(BF16), kv[1])))

    second = lax.rem(s, 2) == 1
    recv("swapk", kvprev.at[0])
    scored = []
    for i in range(4):
        m1, l1, o1 = held[i]
        q = qb[:, i * HD : (i + 1) * HD]
        s0 = jnp.where(second, dot_t(q, kvprev[0]) * scale, NEG)
        m = jnp.maximum(m1, rowmax(s0))
        a1 = jnp.exp(m1 - m)
        e0 = jnp.exp(s0 - m)
        inv = 1.0 / (a1 * l1 + rowsum(e0))
        scored.append((e0.astype(BF16), a1 * o1, inv))
    recv("swapv", kvprev.at[1])
    for i in range(4):
        e0, o1, inv = scored[i]
        o = (o1 + dot(e0, kvprev[1])) * inv
        ctx[c, :, i * HD : (i + 1) * HD] = o.astype(BF16)
        ref = ctx.at[c, :, pl.ds(i * HD, HD)]
        send(("ctx", i), ref, ref, CN)

    @pl.when(mine_parity)
    def _():
        gather_wait(mate_slot)
        for d in range(5, 8):
            gather_copy(d).start()

    far = 1 - yl
    FLOW = (1, 3, 1, 3) * 2
    base = pl.multiple_of(c * 4096, 4096)
    far_base = pl.multiple_of(other * 4096, 4096)

    def width(ci):
        return WA if ci < 4 else WB

    def columns(ci):
        at = ci * WA if ci < 4 else 4 * WA + (ci - 4) * WB
        return slice(at, at + width(ci))

    def rows_of(core):
        return pl.ds(pl.multiple_of(core * 16, 16), 16)

    def along(f):
        return (XP, XM) if f == 1 else (XM, XP)

    def y_first(ci):
        recv(("ry", ci), ray.at[ci])
        parta[ci, yl] = (parta[ci, yl].astype(F32) + ray[ci].astype(F32)).astype(BF16)
        for dx in (2, 1, 3, 0):
            for q in range(2):
                if dx or q:
                    src = parta.at[ci, yl, lax.rem(x + dx, 4), rows_of(lax.rem(c + q, 2))]
                    send(("ax", ci, dx, q), src, rax.at[ci, c, dx], dev(dx, 0, q))

    def x_block(ci, d):
        return partb.at[ci - 4, :, lax.rem(x + d, 4)]

    def x_land(ci, k):
        return rbx.at[ci - 4, k]

    def x_first(ci):
        send(("m1", ci), x_block(ci, 2), x_land(ci, 0), along(FLOW[ci])[0])

    def x_second(ci):
        f = FLOW[ci]
        send(("m2", ci), x_block(ci, 4 - f), x_land(ci, 1), along(f)[1])

    def x_pass(ci):
        f = FLOW[ci]
        recv(("m1", ci), x_land(ci, 0))
        block = x_block(ci, f)
        block[...] = (block[...].astype(F32) + x_land(ci, 0)[...].astype(F32)).astype(BF16)
        send(("m3", ci), block, x_land(ci, 2), along(f)[0])

    def y_last(ci):
        recv(("m2", ci), x_land(ci, 1))
        recv(("m3", ci), x_land(ci, 2))
        land = x_land(ci, 1)
        land[...] = (
            x_block(ci, 0)[...].astype(F32) + land[...].astype(F32) + x_land(ci, 2)[...].astype(F32)
        ).astype(BF16)
        for q in range(2):
            src = land.at[far, rows_of(lax.rem(c + q, 2))]
            send(("by", ci, q), src, rby.at[ci - 4, c], dev(0, 1, q))
        send(("bl", ci), land.at[yl, rows_of(other)], rbl.at[ci - 4], CN)

    def finish(ci):
        at = columns(ci).start
        if ci < 4:
            for dx in range(4):
                for q in range(2):
                    if dx or q:
                        recv(("ax", ci, dx, q), rax.at[ci, lax.rem(c + q, 2), dx])
            near = parta[ci, yl, x, rows_of(c)].astype(F32)
            for dx in range(1, 4):
                near += rax[ci, c, dx].astype(F32)
            away = rax[ci, other, 0].astype(F32)
            for dx in range(1, 4):
                away += rax[ci, other, dx].astype(F32)
        else:
            for q in range(2):
                recv(("by", ci, q), rby.at[ci - 4, lax.rem(c + q, 2)])
            recv(("bl", ci), rbl.at[ci - 4])
            near = rbx[ci - 4, 1, yl, rows_of(c)].astype(F32) + rby[ci - 4, c].astype(F32)
            away = rbl[ci - 4].astype(F32) + rby[ci - 4, other].astype(F32)
        pout[:, pl.ds(base + at, width(ci))] = near.astype(BF16)
        pout[:, pl.ds(far_base + at, width(ci))] = away.astype(BF16)

    def out_own(ci):
        return dot(ctx[c], wo[c, :, columns(ci)])

    def out_rest(ci, total):
        total = (total + dot(ctx[other], wo[other, :, columns(ci)])).astype(BF16)
        if ci < 4:
            parta[ci] = total.reshape(2, 4, 32, WA)
            send(("ry", ci), parta.at[ci, far], ray.at[ci], YN)
        else:
            partb[ci - 4] = total.reshape(2, 4, 32, WB)
            x_first(ci)

    l_wo.wait()
    begun = out_own(7)
    begun_b = out_own(0)
    for i in range(WO_PIECES):
        recv(("wo", i), wo.at[other, pl.ds(i * wo_rows, wo_rows), :])
    for i in range(4):
        recv(("ctx", i), ctx.at[other, :, pl.ds(i * HD, HD)])
    out_rest(7, begun)
    x_second(7)
    out_rest(0, begun_b)
    out_rest(6, out_own(6))
    x_second(6)
    out_rest(2, out_own(2))
    out_rest(5, out_own(5))
    x_second(5)
    out_rest(4, out_own(4))
    x_pass(7)
    for j in range(4):
        @pl.when((2 * j + c != s) & (2 * j + c != mate))
        def _():
            gather_wait(j)

    for r in range(4):
        decode_passage(r)
    send("part", pk, pko, CN)
    x_pass(6)
    x_second(4)
    out_rest(1, out_own(1))
    y_first(0)
    recv("part", pko)
    o1, m1, l1 = pk[0], pk[1, :, 0:1], pk[1, :, 64:65]
    o2, m2, l2 = pko[0], pko[1, :, 0:1], pko[1, :, 64:65]
    mm = jnp.maximum(m1, m2)
    a1, a2 = jnp.exp(m1 - mm), jnp.exp(m2 - mm)
    dec_ctx = ((a1 * o1 + a2 * o2) / (a1 * l1 + a2 * l2)).astype(BF16)
    to = lax.broadcasted_iota(jnp.int32, (16, 64), 0)
    frm = lax.broadcasted_iota(jnp.int32, (16, 64), 1)
    for i in range(4):
        pick = ((to // 4) * 16 + i * 4 + to % 4 == frm).astype(BF16)
        for half in range(2):
            chosen = dot(pick, dec_ctx[half * 64 : half * 64 + 64])
            dctx[half, :, i * HD : (i + 1) * HD] = chosen.astype(BF16)
    for j in range(8):
        cols = slice(j * 512, (j + 1) * 512)
        dpart[j] = (dot(dctx[0], wo[0, :, cols]) + dot(dctx[1], wo[1, :, cols])).astype(BF16)
    for i in (6, 2, 5, 7, 1, 3, 4):
        dx, dy = i % 4, i // 4
        send(("dr", i), dpart.at[chip_at(dx, dy)], dr.at[i], dev(dx, dy))
    y_first(2)
    out_rest(3, out_own(3))
    x_pass(5)
    x_pass(4)
    y_last(6)
    y_first(1)
    total = dpart[chip].astype(F32)
    for i in range(1, 8):
        recv(("dr", i), dr.at[i])
        total = total + dr[i].astype(F32)
    dfull[c, chip] = total.astype(BF16)
    for i in (6, 2, 5, 7, 1, 3, 4):
        dx, dy = i % 4, i // 4
        ref = dfull.at[c, chip]
        send(("db", i), ref, ref, dev(dx, dy))
    y_last(7)
    y_last(4)
    y_first(3)
    finish(0)
    y_last(5)
    for i in range(1, 8):
        dx, dy = i % 4, i // 4
        recv(("db", i), dfull.at[c, chip_at(4 - dx, dy)])
    send("dall", dfull.at[c], dfull.at[c], CN)
    finish(6)
    finish(2)
    finish(1)
    finish(7)
    finish(4)
    finish(3)
    finish(5)

    recv("dall", dfull.at[other])
    for a in range(2):
        for j in range(8):
            at = a * 4096 + j * 512
            dout[:, :, at : at + 512] = dfull[a, j].astype(F32).reshape(4, 4, 512).astype(BF16)

    for cp in sent:
        cp.wait_send()

    @pl.when(mine_parity)
    def _():
        for d in range(1, 8):
            gather_copy(d).wait_send()


def hand_over(p_in, d_in, p_out, d_out):
    p_out[...] = p_in[...]
    d_out[...] = d_in[...]


def local(
    passages, w_query, w_key, w_value, w_out, dec_hidden, cache_keys, cache_values, cache_lengths, assignment
):
    any_spec = pl.BlockSpec(memory_space=pl.ANY)
    smem = pl.BlockSpec(memory_space=pltpu.SMEM)
    vmem = pl.BlockSpec(memory_space=pltpu.VMEM)
    V = pltpu.VMEM
    shapes = (jax.ShapeDtypeStruct((16, 8192), BF16), jax.ShapeDtypeStruct((4, 4, 8192), BF16))
    results = pl.pallas_call(
        kernel,
        out_shape=shapes,
        in_specs=[any_spec] * 8 + [smem] * 2,
        out_specs=(vmem, vmem),
        scratch_shapes=[
            V((8, TOK, 1024), BF16),
            V((8, DEC, 1024), BF16),
            V((8192, 512), BF16),
            V((2 * HD, 8192), BF16),
            V((2, 512, 4096), BF16),
            V((4, 4, 8192), BF16),
            V((4, 1, 2048, HD), BF16),
            V((4, 1, 2048, HD), BF16),
            V((TOK, 512), F32),
            V((TOK, 2 * HD), F32),
            V((DEC, 512), F32),
            V((DEC, 2 * HD), F32),
            V((TOK, 512), BF16),
            V((DEC, 512), BF16),
            V((DEC, 512), BF16),
            V((2, TOK, HD), BF16),
            V((2, TOK, HD), BF16),
            V((4, 2, TOK, HD), BF16),
            V((2, DEC, HD), BF16),
            V((2, TOK, 512), BF16),
            V((4, 2, 4, 32, WA), BF16),
            V((4, 2, 4, 32, WB), BF16),
            V((4, 4, 32, WA), BF16),
            V((4, 2, 4, 16, WA), BF16),
            V((4, 3, 2, 32, WB), BF16),
            V((4, 2, 16, WB), BF16),
            V((4, 16, WB), BF16),
            V((4, 3, 32, HD), F32),
            V((2, 128, HD), F32),
            V((2, 128, HD), F32),
            V((128, HD), BF16),
            V((2, DEC, 512), BF16),
            V((8, DEC, 512), BF16),
            V((8, DEC, 512), BF16),
            V((2, 8, DEC, 512), BF16),
            pltpu.SemaphoreType.DMA((COUNT,)),
            pltpu.SemaphoreType.DMA((COUNT,)),
            pltpu.SemaphoreType.DMA((8,)),
            pltpu.SemaphoreType.DMA((8,)),
            pltpu.SemaphoreType.DMA((4,)),
        ],
        compiler_params=pltpu.CompilerParams(
            collective_id=0, has_side_effects=True, vmem_limit_bytes=60 * 2**20
        ),
        name="layer",
    )(
        passages, w_query, w_key.T, w_value.T, w_out, dec_hidden, cache_keys, cache_values, cache_lengths, assignment
    )
    return pl.pallas_call(
        hand_over,
        out_shape=shapes,
        in_specs=[vmem] * 2,
        out_specs=(vmem, vmem),
        name="hand_over",
    )(*results)


def solution(mesh):
    in_specs = (
        P("seq", "head"),
        P(None, "head"),
        P(None, "head"),
        P(None, "head"),
        P("head", None),
        P("seq", None, None),
        P("seq", "head", None, None),
        P("seq", "head", None, None),
        P("seq"),
        P("seq"),
    )
    out_specs = (P(("seq", "head"), None), P("seq", None, None))
    return jax.shard_map(local, mesh=mesh, in_specs=in_specs, out_specs=out_specs, check_vma=False)
```

```python
import functools
import math

import jax
import jax.numpy as jnp
from jax import lax
from jax.experimental import pallas as pl
from jax.experimental.pallas import tpu as pltpu
from jax.sharding import PartitionSpec as P

MESH = pl.DeviceIdType.MESH
F32 = jnp.float32
BF16 = jnp.bfloat16
HD = 128
TOK = 256
DEC = 16
NEG = -1e30
ROWS = ((0, 64), (64, 48), (112, 64), (176, 80))
HALF = ((0, 112), (112, 144))
WA, WB = 512, 512
WO_PIECES = 8


def message_ids():
    names = []
    for p in range(4):
        names += [("xp", p), ("xm", p), ("y", p)]
    names += [("xpf", 0), ("xpf", 2), ("xmf", 1), ("xmf", 3)]
    names += [("yf", dx, p) for dx in (1, 2, 3) for p in (0, 1)]
    names += [(n, p) for n in ("xpy", "xmy") for p in (2, 3)]
    names += [("xpfy", 2), ("xmfy", 3)]
    names += [("c", dx, dy, a) for dx in range(4) for dy in range(2) for a in range(2)]
    names += [("wo", i) for i in range(WO_PIECES)]
    names += ["wk", "wv", "dq", "swapk", "swapv"]
    names += [("ctx", i) for i in range(4)]
    names += [(n, i) for n in ("m1", "m2", "m3", "bl") for i in range(4, 8)]
    names += [("ry", i) for i in range(4)]
    names += [("ax", i, dx, q) for i in range(4) for dx in range(4) for q in range(2) if dx or q]
    names += [("by", i, q) for i in range(4, 8) for q in range(2)]
    names += ["part", "dall"]
    names += [("dr", i) for i in range(1, 8)] + [("db", i) for i in range(1, 8)]
    return {n: i for i, n in enumerate(names)}


IDS = message_ids()
COUNT = len(IDS)


def dot(a, b):
    return jnp.dot(a, b, preferred_element_type=F32)


def dot_t(a, b):
    return lax.dot_general(a, b, (((1,), (1,)), ((), ())), preferred_element_type=F32)


def rowmax(a):
    return jnp.max(a, axis=1, keepdims=True)


def rowsum(a):
    return jnp.sum(a, axis=1, keepdims=True)


def kernel(
    pas, wq_any, wk_any, wv_any, wo_any, dec_any, ck_any, cv_any, len_ref, asg_ref,
    pout, dout,
    xg, xd, wq, wkv, wo, dech, ck, cv,
    accq, acckv, accdq, accdkv, qb, dqb, dqo, kv, kvprev, kvall, dkv,
    ctx, parta, partb, ray, rax, rbx, rby, rbl,
    pc, pk, pko, qrows, dctx, dpart, dr, dfull,
    ssem, rsem, lsem, gs, gr,
):
    s = lax.axis_index("seq")
    h = lax.axis_index("head")
    c = lax.rem(h, 2)
    other = 1 - c
    chip = lax.div(h, 2)
    x = lax.rem(chip, 4)
    yl = lax.div(chip, 4)
    low = c == 0
    scale = 1.0 / math.sqrt(HD)

    def chip_at(dx, dy):
        return lax.rem(yl + dy, 2) * 4 + lax.rem(x + dx, 4)

    def dev(dx, dy, dc=0):
        return (s, chip_at(dx, dy) * 2 + lax.rem(c + dc, 2))

    XP, XM, YN, CN = dev(1, 0), dev(3, 0), dev(0, 1), dev(0, 0, 1)
    swap_dev = (s + 1 - 2 * lax.rem(s, 2), h)
    mate = lax.rem(s + 4, 8)
    sent = []

    def send(name, src, dst, to):
        m = IDS[name]
        cp = pltpu.make_async_remote_copy(
            src_ref=src, dst_ref=dst, send_sem=ssem.at[m], recv_sem=rsem.at[m],
            device_id=to, device_id_type=MESH,
        )
        cp.start()
        sent.append(cp)

    def recv(name, ref):
        m = IDS[name]
        pltpu.make_async_remote_copy(
            src_ref=ref, dst_ref=ref, send_sem=ssem.at[m], recv_sem=rsem.at[m],
            device_id=CN, device_id_type=MESH,
        ).wait_recv()

    def local(i, src, dst):
        cp = pltpu.make_async_copy(src, dst, lsem.at[i])
        cp.start()
        return cp

    def xs(dx, dy, rows, core):
        return xg.at[
            chip_at(dx, dy), pl.ds(rows[0], rows[1]), pl.ds(pl.multiple_of(core * 512, 512), 512)
        ]

    def kv_rows(i, core):
        return wkv.at[pl.ds(pl.multiple_of(i * HD + core * 64, 64), 64)]

    l_pas = local(0, pas, xs(0, 0, (0, TOK), c))
    l_dec = local(1, dec_any, dech)
    l_wk = local(3, wk_any, kv_rows(0, c))
    l_wv = local(4, wv_any, kv_rows(1, c))
    l_wq = local(2, wq_any, wq)

    barrier = pltpu.get_barrier_semaphore()
    for to in (XP, XM, YN, CN):
        pl.semaphore_signal(barrier, inc=1, device_id=to, device_id_type=MESH)
    z_first = lax.div(s, 4) * 4
    along_z = [z_first + lax.rem(s + d, 4) for d in range(4)]
    for to in along_z[1:] + [mate]:
        pl.semaphore_signal(barrier, inc=1, device_id=(to, h), device_id_type=MESH)
    pl.semaphore_wait(barrier, 8)

    def own(name, p, to):
        send((name, p), pas.at[pl.ds(*ROWS[p])], xs(0, 0, ROWS[p], c), to)

    def fwd(name, dx, dy, rows, to):
        ref = xs(dx, dy, rows, c)
        send(name, ref, ref, to)

    def got(name, dx, dy, rows):
        recv(name, xs(dx, dy, rows, c))

    def share(dx, dy, a):
        fwd(("c", dx, dy, a), dx, dy, HALF[a], CN)

    def shared(dx, dy):
        for a in range(2):
            recv(("c", dx, dy, a), xs(dx, dy, HALF[a], other))

    own("xp", 0, XP)
    own("xm", 1, XM)
    own("y", 2, YN)
    own("xp", 2, XP)
    own("xm", 3, XM)
    own("y", 3, YN)
    own("xp", 1, XP)
    own("xm", 0, XM)
    own("y", 0, YN)
    own("y", 1, YN)
    for a in range(2):
        send(("c", 0, 0, a), pas.at[pl.ds(*HALF[a])], xs(0, 0, HALF[a], c), CN)
    send("wk", wk_any, kv_rows(0, c), CN)
    send("wv", wv_any, kv_rows(1, c), CN)
    l_ck = local(6, ck_any, ck)
    l_cv = local(7, cv_any, cv)
    l_wo = local(5, wo_any.at[:, pl.ds(pl.multiple_of(c * 4096, 4096), 4096)], wo.at[c])

    wo_rows = 512 // WO_PIECES

    def push_wo(i):
        send(
            ("wo", i),
            wo_any.at[pl.ds(i * wo_rows, wo_rows), pl.ds(pl.multiple_of(other * 4096, 4096), 4096)],
            wo.at[c, pl.ds(i * wo_rows, wo_rows), :],
            CN,
        )

    l_dec.wait()
    for j in range(8):
        rows = dech[:, :, j * 1024 : (j + 1) * 1024].astype(F32).reshape(DEC, 1024)
        xd[j] = rows.astype(BF16)
    accq[...] = jnp.zeros_like(accq)
    acckv[...] = jnp.zeros_like(acckv)

    def project_kv(dx, dy):
        j = chip_at(dx, dy)
        cols = pl.ds(pl.multiple_of(j * 1024, 1024), 1024)
        acckv[...] += dot_t(xg[j], wkv[:, cols])

    def project_q(dx, dy):
        j = chip_at(dx, dy)
        rows = pl.ds(pl.multiple_of(j * 1024, 1024), 1024)
        accq[...] += dot(xg[j], wq[rows, :])

    def project(dx, dy):
        shared(dx, dy)
        project_kv(dx, dy)
        project_q(dx, dy)

    def project_new_q(j):
        q = dot(xd[j], wq[j * 1024 : (j + 1) * 1024, :])
        accdq[...] = q if j == 0 else accdq[...] + q

    def project_new_kv(j):
        k = dot_t(xd[j], wkv[:, j * 1024 : (j + 1) * 1024])
        accdkv[...] = k if j == 0 else accdkv[...] + k

    lane = lax.broadcasted_iota(jnp.int32, (16, HD), 1)

    def arrange_new():
        recv("dq", dqo)
        q_low = jnp.where(low, dqb[...].astype(F32), dqo[...].astype(F32)).astype(BF16)
        q_high = jnp.where(low, dqo[...].astype(F32), dqb[...].astype(F32)).astype(BF16)
        q_all = jnp.concatenate(
            [t[:, i * HD : (i + 1) * HD] for t in (q_low, q_high) for i in range(4)], axis=0
        )
        to = lax.broadcasted_iota(jnp.int32, (128, 128), 0)
        frm = lax.broadcasted_iota(jnp.int32, (128, 128), 1)
        source = (to // 64) * 64 + ((to % 16) // 4) * 16 + ((to % 64) // 16) * 4 + to % 4
        qrows[...] = dot((source == frm).astype(BF16), q_all).astype(BF16)
        l_ck.wait()
        l_cv.wait()

    def new_q(r):
        q_rows = qrows[...]
        return jnp.concatenate(
            [q_rows[r * 16 : r * 16 + 16], q_rows[64 + r * 16 : 80 + r * 16]], axis=0
        )

    def decode_cache(r):
        q = new_q(r)
        sc = dot_t(q, ck[r, 0]) * scale
        place = c * 2048 + lax.broadcasted_iota(jnp.int32, sc.shape, 1)
        sc = jnp.where(place < len_ref[r], sc, NEG)
        m = rowmax(sc)
        ec = jnp.exp(sc - m)
        pc[r, 0] = dot(ec.astype(BF16), cv[r, 0])
        pc[r, 1] = jnp.broadcast_to(m, (32, HD))
        pc[r, 2] = jnp.broadcast_to(rowsum(ec), (32, HD))

    def decode_passage():
        held = []
        for r in range(4):
            q = new_q(r)
            pkv = kvall[asg_ref[r]]
            sp = dot_t(q, pkv[0]) * scale
            sn = dot_t(q, dkv[0]) * scale
            step = lax.broadcasted_iota(jnp.int32, sn.shape, 0) % 4
            new = lax.broadcasted_iota(jnp.int32, sn.shape, 1)
            sn = jnp.where(low & (new // 4 == r) & (new % 4 <= step), sn, NEG)
            held.append((sp, sn, pkv[1]))
        for r in range(4):
            sp, sn, values = held[r]
            m1, l1 = pc[r, 1], pc[r, 2]
            m = jnp.maximum(m1, jnp.maximum(rowmax(sp), rowmax(sn)))
            ep, en = jnp.exp(sp - m[:, :1]), jnp.exp(sn - m[:, :1])
            a1 = jnp.exp(m1 - m)
            l = a1 * l1 + rowsum(ep) + rowsum(en)
            held[r] = (ep.astype(BF16), en.astype(BF16), values, a1, m, l)
        for r in range(4):
            ep, en, values, a1, m, l = held[r]
            held[r] = (a1 * pc[r, 0] + dot(ep, values) + dot(en, dkv[1]), m, l)
        for r in range(4):
            o, m, l = held[r]
            for half in range(2):
                t = slice(half * 16, half * 16 + 16)
                at = half * 64 + r * 16
                pk[0, at : at + 16] = o[t]
                pk[1, at : at + 16] = jnp.where(lane < 64, m[t], l[t])

    got(("xm", 1), 1, 0, ROWS[1])
    fwd(("yf", 1, 1), 1, 0, ROWS[1], YN)
    fwd(("xmf", 1), 1, 0, ROWS[1], XM)
    got(("y", 2), 0, 1, ROWS[2])
    fwd(("xpy", 2), 0, 1, ROWS[2], XP)
    got(("xp", 0), 3, 0, ROWS[0])
    fwd(("yf", 3, 0), 3, 0, ROWS[0], YN)
    fwd(("xpf", 0), 3, 0, ROWS[0], XP)
    l_wq.wait()
    for j in range(8):
        project_new_q(j)
    dqb[...] = accdq[...].astype(BF16)
    send("dq", dqb, dqo, CN)
    got(("xp", 2), 3, 0, ROWS[2])
    fwd(("xpf", 2), 3, 0, ROWS[2], XP)
    got(("y", 3), 0, 1, ROWS[3])
    fwd(("xmy", 3), 0, 1, ROWS[3], XM)
    fwd(("xpy", 3), 0, 1, ROWS[3], XP)
    got(("xm", 3), 1, 0, ROWS[3])
    fwd(("xmf", 3), 1, 0, ROWS[3], XM)
    fwd(("xmy", 2), 0, 1, ROWS[2], XM)
    own("xp", 3, XP)
    own("xm", 2, XM)
    share(0, 1, 1)
    arrange_new()
    decode_cache(0)
    got(("xp", 1), 3, 0, ROWS[1])
    fwd(("yf", 3, 1), 3, 0, ROWS[1], YN)
    share(3, 0, 0)
    got(("xm", 0), 1, 0, ROWS[0])
    fwd(("yf", 1, 0), 1, 0, ROWS[0], YN)
    share(1, 0, 0)
    decode_cache(1)
    l_wk.wait()
    l_wv.wait()
    l_pas.wait()
    recv("wk", kv_rows(0, other))
    recv("wv", kv_rows(1, other))
    push_wo(0)
    got(("xpy", 2), 3, 1, ROWS[2])
    fwd(("xpfy", 2), 3, 1, ROWS[2], XP)
    got(("xmf", 1), 2, 0, ROWS[1])
    fwd(("yf", 2, 1), 2, 0, ROWS[1], YN)
    decode_cache(2)
    got(("xpf", 0), 2, 0, ROWS[0])
    fwd(("yf", 2, 0), 2, 0, ROWS[0], YN)
    share(2, 0, 0)
    push_wo(1)
    decode_cache(3)
    got(("xmy", 3), 1, 1, ROWS[3])
    fwd(("xmfy", 3), 1, 1, ROWS[3], XM)
    got(("y", 0), 0, 1, ROWS[0])
    got(("y", 1), 0, 1, ROWS[1])
    share(0, 1, 0)
    for j in range(8):
        project_new_kv(j)
    for i in range(2):
        dkv[i] = accdkv[:, i * HD : (i + 1) * HD].astype(BF16)
    project(0, 0)
    got(("xpf", 2), 2, 0, ROWS[2])
    got(("xmf", 3), 2, 0, ROWS[3])
    share(2, 0, 1)
    push_wo(2)
    project(0, 1)
    got(("yf", 3, 0), 3, 1, ROWS[0])
    got(("yf", 1, 1), 1, 1, ROWS[1])
    got(("yf", 3, 1), 3, 1, ROWS[1])
    got(("yf", 1, 0), 1, 1, ROWS[0])
    share(3, 1, 0)
    share(1, 1, 0)
    got(("xpy", 3), 3, 1, ROWS[3])
    share(3, 1, 1)
    project(2, 0)
    got(("xmy", 2), 1, 1, ROWS[2])
    share(1, 1, 1)
    got(("xp", 3), 3, 0, ROWS[3])
    share(3, 0, 1)
    got(("xm", 2), 1, 0, ROWS[2])
    share(1, 0, 1)
    project(3, 1)
    got(("xpfy", 2), 2, 1, ROWS[2])
    got(("xmfy", 3), 2, 1, ROWS[3])
    share(2, 1, 1)
    got(("yf", 2, 1), 2, 1, ROWS[1])
    got(("yf", 2, 0), 2, 1, ROWS[0])
    share(2, 1, 0)
    project(1, 1)
    last = ((3, 0), (1, 0), (2, 1))
    for place in last:
        shared(*place)
        project_kv(*place)

    for i in range(2):
        kv[i] = acckv[:, i * HD : (i + 1) * HD].astype(BF16)
    send("swapk", kv.at[0], kvprev.at[0], swap_dev)
    send("swapv", kv.at[1], kvprev.at[1], swap_dev)
    mine_parity = lax.rem(s, 2) == c
    slot = lax.div(s, 2)
    mate_slot = lax.div(mate, 2)

    def gather_copy(d):
        to = mate if d == 4 else along_z[d % 4]
        if d < 5:
            src, at = kv, slot
        else:
            src, at = kvall.at[mate_slot], mate_slot
        return pltpu.make_async_remote_copy(
            src_ref=src, dst_ref=kvall.at[at], send_sem=gs.at[d], recv_sem=gr.at[at],
            device_id=(to, h), device_id_type=MESH,
        )

    def gather_wait(j):
        pltpu.make_async_remote_copy(
            src_ref=kv, dst_ref=kvall.at[j], send_sem=gs.at[0], recv_sem=gr.at[j],
            device_id=CN, device_id_type=MESH,
        ).wait_recv()

    @pl.when(mine_parity)
    def _():
        gather_copy(4).start()
        for d in range(1, 4):
            gather_copy(d).start()
        kvall[slot] = kv[...]

    for i in range(3, WO_PIECES):
        push_wo(i)
    for place in last:
        project_q(*place)
    qb[...] = accq[...].astype(BF16)

    row = lax.broadcasted_iota(jnp.int32, (TOK, TOK), 0)
    col = lax.broadcasted_iota(jnp.int32, (TOK, TOK), 1)
    held = []
    for i in range(4):
        q = qb[:, i * HD : (i + 1) * HD]
        s1 = jnp.where(row >= col, dot_t(q, kv[0]) * scale, NEG)
        m1 = rowmax(s1)
        e1 = jnp.exp(s1 - m1)
        held.append((m1, rowsum(e1), dot(e1.astype(BF16), kv[1])))

    second = lax.rem(s, 2) == 1
    recv("swapk", kvprev.at[0])
    scored = []
    for i in range(4):
        m1, l1, o1 = held[i]
        q = qb[:, i * HD : (i + 1) * HD]
        s0 = jnp.where(second, dot_t(q, kvprev[0]) * scale, NEG)
        m = jnp.maximum(m1, rowmax(s0))
        a1 = jnp.exp(m1 - m)
        e0 = jnp.exp(s0 - m)
        inv = 1.0 / (a1 * l1 + rowsum(e0))
        scored.append((e0.astype(BF16), a1 * o1, inv))
    recv("swapv", kvprev.at[1])
    for i in range(4):
        e0, o1, inv = scored[i]
        o = (o1 + dot(e0, kvprev[1])) * inv
        ctx[c, :, i * HD : (i + 1) * HD] = o.astype(BF16)
        ref = ctx.at[c, :, pl.ds(i * HD, HD)]
        send(("ctx", i), ref, ref, CN)

    @pl.when(mine_parity)
    def _():
        gather_wait(mate_slot)
        for d in range(5, 8):
            gather_copy(d).start()

    far = 1 - yl
    FLOW = (1, 3, 1, 3) * 2
    base = pl.multiple_of(c * 4096, 4096)
    far_base = pl.multiple_of(other * 4096, 4096)

    def width(ci):
        return WA if ci < 4 else WB

    def columns(ci):
        at = ci * WA if ci < 4 else 4 * WA + (ci - 4) * WB
        return slice(at, at + width(ci))

    def rows_of(core):
        return pl.ds(pl.multiple_of(core * 16, 16), 16)

    def along(f):
        return (XP, XM) if f == 1 else (XM, XP)

    def y_first(ci):
        recv(("ry", ci), ray.at[ci])
        parta[ci, yl] = (parta[ci, yl].astype(F32) + ray[ci].astype(F32)).astype(BF16)
        for dx in (2, 1, 3, 0):
            for q in range(2):
                if dx or q:
                    src = parta.at[ci, yl, lax.rem(x + dx, 4), rows_of(lax.rem(c + q, 2))]
                    send(("ax", ci, dx, q), src, rax.at[ci, c, dx], dev(dx, 0, q))

    def x_block(ci, d):
        return partb.at[ci - 4, :, lax.rem(x + d, 4)]

    def x_land(ci, k):
        return rbx.at[ci - 4, k]

    def x_first(ci):
        send(("m1", ci), x_block(ci, 2), x_land(ci, 0), along(FLOW[ci])[0])

    def x_second(ci):
        f = FLOW[ci]
        send(("m2", ci), x_block(ci, 4 - f), x_land(ci, 1), along(f)[1])

    def x_pass(ci):
        f = FLOW[ci]
        recv(("m1", ci), x_land(ci, 0))
        block = x_block(ci, f)
        block[...] = (block[...].astype(F32) + x_land(ci, 0)[...].astype(F32)).astype(BF16)
        send(("m3", ci), block, x_land(ci, 2), along(f)[0])

    def y_last(ci):
        recv(("m2", ci), x_land(ci, 1))
        recv(("m3", ci), x_land(ci, 2))
        land = x_land(ci, 1)
        land[...] = (
            x_block(ci, 0)[...].astype(F32) + land[...].astype(F32) + x_land(ci, 2)[...].astype(F32)
        ).astype(BF16)
        for q in range(2):
            src = land.at[far, rows_of(lax.rem(c + q, 2))]
            send(("by", ci, q), src, rby.at[ci - 4, c], dev(0, 1, q))
        send(("bl", ci), land.at[yl, rows_of(other)], rbl.at[ci - 4], CN)

    def finish(ci):
        at = columns(ci).start
        if ci < 4:
            for dx in range(4):
                for q in range(2):
                    if dx or q:
                        recv(("ax", ci, dx, q), rax.at[ci, lax.rem(c + q, 2), dx])
            near = parta[ci, yl, x, rows_of(c)].astype(F32)
            for dx in range(1, 4):
                near += rax[ci, c, dx].astype(F32)
            away = rax[ci, other, 0].astype(F32)
            for dx in range(1, 4):
                away += rax[ci, other, dx].astype(F32)
        else:
            for q in range(2):
                recv(("by", ci, q), rby.at[ci - 4, lax.rem(c + q, 2)])
            recv(("bl", ci), rbl.at[ci - 4])
            near = rbx[ci - 4, 1, yl, rows_of(c)].astype(F32) + rby[ci - 4, c].astype(F32)
            away = rbl[ci - 4].astype(F32) + rby[ci - 4, other].astype(F32)
        pout[:, pl.ds(base + at, width(ci))] = near.astype(BF16)
        pout[:, pl.ds(far_base + at, width(ci))] = away.astype(BF16)

    def out_own(ci):
        return dot(ctx[c], wo[c, :, columns(ci)])

    def out_rest(ci, total):
        total = (total + dot(ctx[other], wo[other, :, columns(ci)])).astype(BF16)
        if ci < 4:
            parta[ci] = total.reshape(2, 4, 32, WA)
            send(("ry", ci), parta.at[ci, far], ray.at[ci], YN)
        else:
            partb[ci - 4] = total.reshape(2, 4, 32, WB)
            x_first(ci)

    l_wo.wait()
    begun = out_own(7)
    begun_b = out_own(0)
    for i in range(WO_PIECES):
        recv(("wo", i), wo.at[other, pl.ds(i * wo_rows, wo_rows), :])
    for i in range(4):
        recv(("ctx", i), ctx.at[other, :, pl.ds(i * HD, HD)])
    out_rest(7, begun)
    x_second(7)
    out_rest(0, begun_b)
    out_rest(6, out_own(6))
    x_second(6)
    out_rest(2, out_own(2))
    out_rest(5, out_own(5))
    x_second(5)
    out_rest(4, out_own(4))
    x_pass(7)
    for j in range(4):
        @pl.when((2 * j + c != s) & (2 * j + c != mate))
        def _():
            gather_wait(j)

    decode_passage()
    send("part", pk, pko, CN)
    x_pass(6)
    x_second(4)
    out_rest(1, out_own(1))
    y_first(0)
    recv("part", pko)
    o1, m1, l1 = pk[0], pk[1, :, 0:1], pk[1, :, 64:65]
    o2, m2, l2 = pko[0], pko[1, :, 0:1], pko[1, :, 64:65]
    mm = jnp.maximum(m1, m2)
    a1, a2 = jnp.exp(m1 - mm), jnp.exp(m2 - mm)
    dec_ctx = ((a1 * o1 + a2 * o2) / (a1 * l1 + a2 * l2)).astype(BF16)
    to = lax.broadcasted_iota(jnp.int32, (16, 64), 0)
    frm = lax.broadcasted_iota(jnp.int32, (16, 64), 1)
    for i in range(4):
        pick = ((to // 4) * 16 + i * 4 + to % 4 == frm).astype(BF16)
        for half in range(2):
            chosen = dot(pick, dec_ctx[half * 64 : half * 64 + 64])
            dctx[half, :, i * HD : (i + 1) * HD] = chosen.astype(BF16)
    for j in range(8):
        cols = slice(j * 512, (j + 1) * 512)
        dpart[j] = (dot(dctx[0], wo[0, :, cols]) + dot(dctx[1], wo[1, :, cols])).astype(BF16)
    for i in (6, 2, 5, 7, 1, 3, 4):
        dx, dy = i % 4, i // 4
        send(("dr", i), dpart.at[chip_at(dx, dy)], dr.at[i], dev(dx, dy))
    y_first(2)
    out_rest(3, out_own(3))
    x_pass(5)
    x_pass(4)
    y_last(6)
    y_first(1)
    total = dpart[chip].astype(F32)
    for i in range(1, 8):
        recv(("dr", i), dr.at[i])
        total = total + dr[i].astype(F32)
    dfull[c, chip] = total.astype(BF16)
    for i in (6, 2, 5, 7, 1, 3, 4):
        dx, dy = i % 4, i // 4
        ref = dfull.at[c, chip]
        send(("db", i), ref, ref, dev(dx, dy))
    y_last(7)
    y_last(4)
    y_first(3)
    finish(0)
    y_last(5)
    for i in range(1, 8):
        dx, dy = i % 4, i // 4
        recv(("db", i), dfull.at[c, chip_at(4 - dx, dy)])
    send("dall", dfull.at[c], dfull.at[c], CN)
    finish(6)
    finish(2)
    finish(1)
    finish(7)
    finish(4)
    finish(3)
    finish(5)

    recv("dall", dfull.at[other])
    for a in range(2):
        for j in range(8):
            at = a * 4096 + j * 512
            dout[:, :, at : at + 512] = dfull[a, j].astype(F32).reshape(4, 4, 512).astype(BF16)

    for cp in sent:
        cp.wait_send()

    @pl.when(mine_parity)
    def _():
        for d in range(1, 8):
            gather_copy(d).wait_send()


def hand_over(p_in, d_in, p_out, d_out):
    p_out[...] = p_in[...]
    d_out[...] = d_in[...]


def local(
    passages, w_query, w_key, w_value, w_out, dec_hidden, cache_keys, cache_values, cache_lengths, assignment
):
    any_spec = pl.BlockSpec(memory_space=pl.ANY)
    smem = pl.BlockSpec(memory_space=pltpu.SMEM)
    vmem = pl.BlockSpec(memory_space=pltpu.VMEM)
    V = pltpu.VMEM
    shapes = (jax.ShapeDtypeStruct((16, 8192), BF16), jax.ShapeDtypeStruct((4, 4, 8192), BF16))
    results = pl.pallas_call(
        kernel,
        out_shape=shapes,
        in_specs=[any_spec] * 8 + [smem] * 2,
        out_specs=(vmem, vmem),
        scratch_shapes=[
            V((8, TOK, 1024), BF16),
            V((8, DEC, 1024), BF16),
            V((8192, 512), BF16),
            V((2 * HD, 8192), BF16),
            V((2, 512, 4096), BF16),
            V((4, 4, 8192), BF16),
            V((4, 1, 2048, HD), BF16),
            V((4, 1, 2048, HD), BF16),
            V((TOK, 512), F32),
            V((TOK, 2 * HD), F32),
            V((DEC, 512), F32),
            V((DEC, 2 * HD), F32),
            V((TOK, 512), BF16),
            V((DEC, 512), BF16),
            V((DEC, 512), BF16),
            V((2, TOK, HD), BF16),
            V((2, TOK, HD), BF16),
            V((4, 2, TOK, HD), BF16),
            V((2, DEC, HD), BF16),
            V((2, TOK, 512), BF16),
            V((4, 2, 4, 32, WA), BF16),
            V((4, 2, 4, 32, WB), BF16),
            V((4, 4, 32, WA), BF16),
            V((4, 2, 4, 16, WA), BF16),
            V((4, 3, 2, 32, WB), BF16),
            V((4, 2, 16, WB), BF16),
            V((4, 16, WB), BF16),
            V((4, 3, 32, HD), F32),
            V((2, 128, HD), F32),
            V((2, 128, HD), F32),
            V((128, HD), BF16),
            V((2, DEC, 512), BF16),
            V((8, DEC, 512), BF16),
            V((8, DEC, 512), BF16),
            V((2, 8, DEC, 512), BF16),
            pltpu.SemaphoreType.DMA((COUNT,)),
            pltpu.SemaphoreType.DMA((COUNT,)),
            pltpu.SemaphoreType.DMA((8,)),
            pltpu.SemaphoreType.DMA((8,)),
            pltpu.SemaphoreType.DMA((4,)),
        ],
        compiler_params=pltpu.CompilerParams(
            collective_id=0, has_side_effects=True, vmem_limit_bytes=60 * 2**20
        ),
        name="layer",
    )(
        passages, w_query, w_key.T, w_value.T, w_out, dec_hidden, cache_keys, cache_values, cache_lengths, assignment
    )
    return pl.pallas_call(
        hand_over,
        out_shape=shapes,
        in_specs=[vmem] * 2,
        out_specs=(vmem, vmem),
        name="hand_over",
    )(*results)


def solution(mesh):
    in_specs = (
        P("seq", "head"),
        P(None, "head"),
        P(None, "head"),
        P(None, "head"),
        P("head", None),
        P("seq", None, None),
        P("seq", "head", None, None),
        P("seq", "head", None, None),
        P("seq"),
        P("seq"),
    )
    out_specs = (P(("seq", "head"), None), P("seq", None, None))
    return jax.shard_map(local, mesh=mesh, in_specs=in_specs, out_specs=out_specs, check_vma=False)
```
